256 devices in a mesh: sky: 32 (over z, y), grp: 8 (over x, core).
Axes of the slice: x: 4, y: 4, z: 8, core: 2. Of those that a mesh axis runs over, the one named last changes fastest.
Arguments:
- pixels: float32 [8, 2048, 16, 512], P('grp', 'sky'), may hold values from -6 to 6
- mask_bits: int32 [8, 2048, 512], P('grp', 'sky'), may hold values from 0 to 7, as said below
- owner: int32 [8, 2048], P('grp', 'sky'), may hold values from 0 to 31, as said below
- row_offset: int32 [8, 2048], P('grp', 'sky'), may hold values from 0 to 48
- seg_weight: float32 [8, 2048], P('grp', 'sky'), may hold values from 0.01 to 0.2
- psf_bank: float32 [8, 2, 21], replicated, may hold values from -1.25 to 1.25
- basis_index: int32 [8, 3], P('grp'), may hold values from 0 to 7
- basis_coeff: float32 [8, 3], P('grp'), may hold values from -3 to 3
- row_base: int32 [8, 16], P('grp'), may hold values from 0 to 14
- row_frac: float32 [8, 16], P('grp'), may hold values from 0 to 1
- col_base: int32 [8, 512], P('grp'), may hold values from 0 to 510
- col_frac: float32 [8, 512], P('grp'), may hold values from 0 to 1
Outputs:
- coadd: float32 [2048, 512], P(('sky', 'grp'))
The draws below stay inside these ranges and needn't reach their ends.
Inputs may be any that keep to these rules, and one draw needn't show every extreme that they name: Each device of an exposure group holds at most 8 segments of one owner; in each exposure one owner holds exactly 8 segments in every aligned block of 64 segments. `mask_bits`: bit 0 marks bad columns, bit 1 saturated ones, bit 2 cosmic-ray hits.
All inputs are finite; a program needn't handle non-finite values.
Results may differ from the reference program's by a relative error of at most 0.00012.
Values sent between devices are 32-bit elements; how exact they have to be, the bound alone decides.
No kernel may reach another device: no remote copies, remote signals or barrier semaphores. Data moves between devices by JAX's collectives and lax.ppermute only.
A program may use at most 128 MiB of HBM per device.

```python
import math
import jax
import jax.numpy as jnp
from jax import lax

WIDTH = 512
TAPS = 21
NBASIS = 3
NBANK = 8
ROWS = 16
PATCH = 64
SEG_DEV = 64
CAP = 8
SEGMENTS = 2048
EXPOSURES = 8
N_SKY = 32
N_GRP = 8


def draw_owner(key, part):
    key = jax.random.fold_in(key, 11)
    hot_key, pick_key, order_key = jax.random.split(key, 3)
    hottest = jax.random.randint(hot_key, (N_GRP,), 0, N_SKY).astype(jnp.int32)
    blocks = N_GRP * N_SKY
    pool = (jnp.arange((N_SKY - 1) * CAP, dtype=jnp.int32) // CAP).astype(jnp.int32)
    pick_keys = jax.random.split(pick_key, blocks)
    order_keys = jax.random.split(order_key, blocks)
    hot_rows = jnp.repeat(hottest, N_SKY)

    def one_block(pick_one, order_one, hot_one):
        chosen = jax.random.permutation(pick_one, pool)[:SEG_DEV - CAP]
        chosen = chosen + (chosen >= hot_one).astype(jnp.int32)
        whole = jnp.concatenate([jnp.full((CAP,), hot_one, jnp.int32), chosen])
        return jax.random.permutation(order_one, whole)
    table = jax.vmap(one_block)(pick_keys, order_keys, hot_rows)
    return table.reshape(N_GRP, N_SKY * SEG_DEV).astype(jnp.int32)


def draw_mask_bits(key, part):
    key = jax.random.fold_in(key, 23)
    planes = jax.random.randint(key, (3, N_GRP, N_SKY * SEG_DEV, WIDTH), 0, 6)
    flags = (planes == 0).astype(jnp.int32)
    return (flags[0] + 2 * flags[1] + 4 * flags[2]).astype(jnp.int32)


def with_ends(array, rng, low, top_value):
    longest = array.shape.index(max(array.shape))
    spots = []
    for shift in (0, 1):
        where = [jax.random.randint(jax.random.fold_in(rng, axis), (), 0, length) for axis, length in enumerate(array.shape)]
        where[longest] = (where[longest] + shift) % array.shape[longest]
        spots.append(tuple(where))
    return array.at[spots[0]].set(low).at[spots[1]].set(top_value)


def level_of(own_key, extent, cuts, least, high):
    def one(position, parts):
        steps = jax.random.uniform(jax.random.fold_in(jax.random.fold_in(own_key, 6), position), (parts,), jnp.float32, least / len(cuts), high / len(cuts))
        return jnp.repeat(jnp.exp(steps), extent[position] // parts).reshape((-1,) + (1,) * (len(extent) - position - 1))

    gain = one(*cuts[0])
    for cut in cuts[1:]:
        gain = gain * one(*cut)
    return gain


def normal_values(own_key, dims, scale, bound, cuts=(), kind=jnp.bfloat16):
    values = jax.random.normal(own_key, dims, jnp.float32) * scale
    if len(cuts) > 0:
        values = level_of(own_key, dims, cuts, -0.22, 0.18) * values
    return jnp.clip(values, min=-bound, max=bound).astype(kind)


def setup_inputs(seed: int = 0) -> dict:
    seeds = jax.random.split(jax.random.key(seed), 13)
    return {
        "pixels": normal_values(seeds[0], (EXPOSURES, SEGMENTS, ROWS, WIDTH), 1.0, 6.0, ((0, 8), (1, 32)), jnp.float32),
        "mask_bits": draw_mask_bits(jax.random.fold_in(seeds[12], 71), 0),
        "owner": draw_owner(jax.random.fold_in(seeds[12], 71), 0),
        "row_offset": with_ends(jax.random.randint(seeds[3], (EXPOSURES, SEGMENTS), 0, PATCH - ROWS + 1), jax.random.fold_in(seeds[3], 1), 0, PATCH - ROWS).astype(jnp.int32),
        "seg_weight": jnp.clip(jnp.exp(math.log(0.2) - 2.9957323 * jax.random.uniform(seeds[4], (EXPOSURES, SEGMENTS), jnp.float32) ** level_of(seeds[4], (EXPOSURES, SEGMENTS), ((0, 8), (1, 32)), -0.2, 0.2)), 0.01, 0.2),
        "psf_bank": normal_values(seeds[5], (NBANK, 2, TAPS), TAPS ** -0.5, 1.25, (), jnp.float32),
        "basis_index": with_ends(jax.random.randint(seeds[6], (EXPOSURES, NBASIS), 0, NBANK), jax.random.fold_in(seeds[6], 1), 0, NBANK - 1).astype(jnp.int32),
        "basis_coeff": normal_values(seeds[7], (EXPOSURES, NBASIS), 0.6, 3.0, ((0, 8),), jnp.float32),
        "row_base": with_ends(jax.random.randint(seeds[8], (EXPOSURES, ROWS), 0, ROWS - 1), jax.random.fold_in(seeds[8], 1), 0, (ROWS - 1) - 1).astype(jnp.int32),
        "row_frac": jnp.clip(1.0 * jax.random.uniform(seeds[9], (EXPOSURES, ROWS), jnp.float32) ** level_of(seeds[9], (EXPOSURES, ROWS), ((0, 8),), -0.2, 0.2), 0.0, 1.0),
        "col_base": with_ends(jax.random.randint(seeds[10], (EXPOSURES, WIDTH), 0, WIDTH - 1), jax.random.fold_in(seeds[10], 1), 0, (WIDTH - 1) - 1).astype(jnp.int32),
        "col_frac": jnp.clip(1.0 * jax.random.uniform(seeds[11], (EXPOSURES, WIDTH), jnp.float32) ** level_of(seeds[11], (EXPOSURES, WIDTH), ((0, 8),), -0.2, 0.2), 0.0, 1.0),
    }


highest = lax.Precision.HIGHEST


def taps_matrix(profile, offsets):
    result = jnp.zeros(offsets.shape, jnp.float32)
    for tap_index in range(profile.shape[0]):
        result = result + profile[tap_index] * (offsets == tap_index).astype(jnp.float32)
    return result


def warp_matrix(base_index, fraction, length):
    source = jnp.arange(length, dtype=jnp.int32)[:, None]
    lower = (source == base_index[None, :]).astype(jnp.float32)
    higher = (source == base_index[None, :] + 1).astype(jnp.float32)
    return (1.0 - fraction)[None, :] * lower + fraction[None, :] * higher


def column_factor(mask_bits):
    bad_flag = (mask_bits % 2).astype(jnp.float32)
    full_flag = ((mask_bits // 2) % 2).astype(jnp.float32)
    cosmic_flag = ((mask_bits // 4) % 2).astype(jnp.float32)
    return (1.0 - bad_flag) * (1.0 - 0.75 * full_flag) * (1.0 - 0.5 * cosmic_flag)


def exposure_tables(psf_bank, basis_index, row_base, row_frac, col_base, col_frac, strip_rows, strip_width):
    bank_lead = jnp.arange(psf_bank.shape[0], dtype=jnp.int32)
    picker = (basis_index[:, None] == bank_lead[None, :]).astype(jnp.float32)
    profiles = jnp.einsum("kb,bst->kst", picker, psf_bank, precision=highest)
    reach = (psf_bank.shape[2] - 1) // 2
    row_lead = jnp.arange(strip_rows, dtype=jnp.int32)
    col_lead = jnp.arange(strip_width, dtype=jnp.int32)
    column_warp = warp_matrix(col_base, col_frac, strip_width)
    row_warp = warp_matrix(row_base, row_frac, strip_rows).T
    row_list = []
    col_list = []
    for basis_term in range(profiles.shape[0]):
        row_list.append(taps_matrix(profiles[basis_term, 0], row_lead[None, :] - row_lead[:, None] + reach))
        banded = taps_matrix(profiles[basis_term, 1], col_lead[:, None] - col_lead[None, :] + reach)
        col_list.append(jnp.dot(banded, column_warp, precision=highest))
    return jnp.stack(row_list), jnp.stack(col_list), column_warp, row_warp


def match_psf(images, factors, row_mats, col_mats, coeffs, column_warp):
    result = jnp.zeros(images.shape, jnp.float32)
    for basis_term in range(row_mats.shape[0]):
        row_pass = jnp.einsum("ia,naw->niw", row_mats[basis_term], images, precision=highest)
        result = result + coeffs[basis_term] * jnp.einsum("niw,wj->nij", row_pass, col_mats[basis_term], precision=highest)
    coverage = jnp.dot(factors, column_warp, precision=highest)
    return result, coverage


def reference(pixels, mask_bits, owner, row_offset, seg_weight, psf_bank, basis_index, basis_coeff, row_base, row_frac, col_base, col_frac):
    numer = jnp.zeros((N_SKY * PATCH, WIDTH), jnp.float32)
    denom = jnp.zeros((N_SKY * PATCH, WIDTH), jnp.float32)
    for exposure in range(N_GRP):
        row_mats, col_mats, column_warp, row_warp = exposure_tables(psf_bank, basis_index[exposure], row_base[exposure], row_frac[exposure], col_base[exposure], col_frac[exposure], ROWS, WIDTH)
        factors = column_factor(mask_bits[exposure])
        masked = pixels[exposure] * factors[:, None, :]
        matched, coverage = match_psf(masked, factors, row_mats, col_mats, basis_coeff[exposure], column_warp)
        weights = seg_weight[exposure]
        lifted = jnp.einsum("ia,naw->niw", row_warp, matched, precision=highest) * weights[:, None, None]
        spread = jnp.sum(row_warp, axis=1)
        starts = owner[exposure] * PATCH + row_offset[exposure]
        targets = (starts[:, None] + jnp.arange(ROWS, dtype=jnp.int32)[None, :]).reshape(-1).astype(jnp.int32)
        numer = numer.at[targets].add(lifted.reshape(-1, WIDTH))
        weight_rows = weights[:, None] * spread[None, :]
        denom = denom.at[targets].add((weight_rows[:, :, None] * coverage[:, None, :]).reshape(-1, WIDTH))
    return numer / jnp.maximum(denom, 1.0)
```

```python
import functools

import jax
import jax.numpy as jnp
from jax import lax
from jax.experimental import pallas as pl
from jax.experimental.pallas import tpu as pltpu
from jax.sharding import PartitionSpec as P

F32 = jnp.float32
BF16 = jnp.bfloat16
NX, NY, NZ = 4, 4, 8
SEGS = 64
ROWS = 16
WIDTH = 512
TAPS = 21
REACH = 10
NBASIS = 3
LANES = 128
BLOCKS = WIDTH // LANES
BLOCK_SEGS = 16
BLOCK_ROWS = BLOCK_SEGS * ROWS


def split(value):
    high = value.astype(BF16)
    return high, (value - high.astype(F32)).astype(BF16)


def column_factor(bits):
    bad = (bits & 1).astype(F32)
    full = ((bits >> 1) & 1).astype(F32)
    cosmic = ((bits >> 2) & 1).astype(F32)
    return (1.0 - bad) * (1.0 - 0.75 * full) * (1.0 - 0.5 * cosmic)


def column_warp(base_ref, frac_ref):
    source = lax.broadcasted_iota(jnp.int32, (WIDTH, WIDTH), 0)
    base = base_ref[...]
    frac = frac_ref[...]
    return jnp.where(source == base, 1.0 - frac, 0.0) + jnp.where(source == base + 1, frac, 0.0)


def column_of(ref, shape):
    row = lax.broadcasted_iota(jnp.int32, shape, 0)
    result = jnp.full(shape, ref[0, 0])
    for i in range(1, ROWS):
        result = jnp.where(row == i, ref[0, i], result)
    return result


def relative_patch(place_ref, owner):
    ry = (owner % NY - place_ref[2] + NY) % NY
    rz = (owner // NY - place_ref[3] + NZ) % NZ
    return ry, rz


def write_out(place_ref, sums, outs, sems):
    keep_x, send_x, keep_y, send_y = outs
    copies = []
    for rc, (to_x, to_y) in enumerate(((keep_x, keep_y), (send_x, send_y))):
        core = (place_ref[0] + rc) % 2
        for rx in range(NX):
            tile = ((place_ref[1] + rx) % NX) * 2 + core
            rows = pl.ds(pl.multiple_of(tile * 8, 8), 8)
            for block in range(2):
                copies.append((sums.at[block, :, :, rows, :], to_x.at[rx, block]))
                copies.append((sums.at[2 + block, :, :, rows, :], to_y.at[:, rx, block]))
    started = [pltpu.make_async_copy(src, dst, sems.at[i]) for i, (src, dst) in enumerate(copies)]
    for copy in started:
        copy.start()
    for copy in started:
        copy.wait()


def denom_kernel(
    place_ref, owner_ref, offset_ref, weight_ref, frac_ref, bits_ref, col_base_ref, col_frac_ref,
    keep_x, send_x, keep_y, send_y, sums, cover, sems,
):
    factor = column_factor(bits_ref[0]).astype(BF16)
    warp_high, warp_low = split(column_warp(col_base_ref, col_frac_ref))
    coverage = jnp.dot(factor, warp_high, preferred_element_type=F32) + jnp.dot(
        factor, warp_low, preferred_element_type=F32
    )
    for block in range(BLOCKS):
        cover[block] = coverage[:, block * LANES : (block + 1) * LANES]
    frac = column_of(frac_ref, (ROWS, LANES))
    spread = (1.0 - frac) + frac
    sums[...] = jnp.zeros(sums.shape, F32)

    def one(s, carry):
        ry, rz = relative_patch(place_ref, owner_ref[0, s])
        rows = pl.ds(offset_ref[0, s], ROWS)
        share = spread * weight_ref[0, s]
        for block in range(BLOCKS):
            sums[block, ry, rz, rows, :] += share * cover[block, pl.ds(s, 1), :]
        return carry

    lax.fori_loop(0, SEGS, one, 0, unroll=2)
    write_out(place_ref, sums, (keep_x, send_x, keep_y, send_y), sems)


def row_tables(bank_ref, index_ref, coeff_ref, base_ref, frac_ref, k):
    shape = (ROWS, BLOCK_ROWS)
    delta = lax.broadcasted_iota(jnp.int32, shape, 1) % ROWS - column_of(base_ref, shape) + REACH
    frac = column_of(frac_ref, shape)
    term = index_ref[0, k]
    lower = jnp.zeros(shape, F32)
    higher = jnp.zeros(shape, F32)
    for tap in range(TAPS):
        value = bank_ref[term, 0, tap]
        lower = jnp.where(delta == tap, value, lower)
        higher = jnp.where(delta == tap + 1, value, higher)
    return ((1.0 - frac) * lower + frac * higher) * coeff_ref[0, k]


def band_tables(bank_ref, index_ref, k):
    lane = lax.broadcasted_iota(jnp.int32, (LANES, WIDTH), 1)
    term = index_ref[0, k]
    base = jnp.zeros((LANES, WIDTH), F32)
    for tap in range(TAPS):
        base = jnp.where(lane == LANES + REACH - tap, bank_ref[term, 1, tap], base)
    return pltpu.roll(base, 0, 1, stride=1, stride_axis=0)[:, : 3 * LANES]


def rows_kernel(
    bank_ref, index_ref, coeff_ref, base_ref, frac_ref, bits_ref, pixels_ref, u_high, u_low, blockdiag
):
    same = (
        lax.broadcasted_iota(jnp.int32, (BLOCK_ROWS, BLOCK_ROWS), 0) // ROWS
        == lax.broadcasted_iota(jnp.int32, (BLOCK_ROWS, BLOCK_ROWS), 1) // ROWS
    )
    for k in range(NBASIS):
        table = row_tables(bank_ref, index_ref, coeff_ref, base_ref, frac_ref, k)
        whole = jnp.where(same, jnp.concatenate([table] * BLOCK_SEGS, axis=0), 0.0)
        high, low = split(whole)
        rows = slice(k * BLOCK_ROWS, (k + 1) * BLOCK_ROWS)
        blockdiag[rows, 0:BLOCK_ROWS] = high
        blockdiag[rows, BLOCK_ROWS : 2 * BLOCK_ROWS] = high
        blockdiag[rows, 2 * BLOCK_ROWS :] = low

    def one(b, carry):
        segs = pl.ds(b * BLOCK_SEGS, BLOCK_SEGS)
        factor = column_factor(bits_ref[0, segs, :])
        masked = (pixels_ref[0, segs] * factor[:, None, :]).reshape(BLOCK_ROWS, WIDTH)
        high, low = split(masked)
        product = jnp.dot(
            blockdiag[...], jnp.concatenate([high, low, high], axis=0), preferred_element_type=F32
        )
        rows = pl.ds(pl.multiple_of(b * BLOCK_ROWS, BLOCK_ROWS), BLOCK_ROWS)
        for k in range(NBASIS):
            part_high, part_low = split(product[k * BLOCK_ROWS : (k + 1) * BLOCK_ROWS])
            u_high[rows, k * WIDTH : (k + 1) * WIDTH] = part_high
            u_low[rows, k * WIDTH : (k + 1) * WIDTH] = part_low
        return carry

    lax.fori_loop(0, SEGS // BLOCK_SEGS, one, 0)


def numer_kernel(
    place_ref, owner_ref, offset_ref, weight_ref, bank_ref, index_ref, col_base_ref, col_frac_ref, u_high, u_low,
    keep_x, send_x, keep_y, send_y, sums, lifted, band_high, band_low, warp_high, warp_low, sems,
):
    band_high[...] = jnp.zeros(band_high.shape, BF16)
    band_low[...] = jnp.zeros(band_low.shape, BF16)
    for k in range(NBASIS):
        high, low = split(band_tables(bank_ref, index_ref, k))
        for block in range(BLOCKS):
            first = max(block - 1, 0)
            last = min(block + 1, BLOCKS - 1)
            rows = slice(k * WIDTH + block * LANES, k * WIDTH + (block + 1) * LANES)
            to = slice(first * LANES, (last + 1) * LANES)
            of = slice((first - block + 1) * LANES, (last - block + 2) * LANES)
            band_high[rows, to] = high[:, of]
            band_low[rows, to] = low[:, of]
    high, low = split(column_warp(col_base_ref, col_frac_ref))
    warp_high[...] = high
    warp_low[...] = low
    sums[...] = jnp.zeros(sums.shape, F32)
    dot = functools.partial(jnp.dot, preferred_element_type=F32)

    def one(b, carry):
        rows = pl.ds(pl.multiple_of(b * BLOCK_ROWS, BLOCK_ROWS), BLOCK_ROWS)
        part_high = u_high[rows, :]
        part_low = u_low[rows, :]
        wide = dot(part_high, band_high[...]) + dot(part_high, band_low[...]) + dot(part_low, band_high[...])
        high, low = split(wide)
        warped = dot(high, warp_high[...]) + dot(high, warp_low[...]) + dot(low, warp_high[...])
        for block in range(BLOCKS):
            lifted[block, rows, :] = warped[:, block * LANES : (block + 1) * LANES]
        return carry

    lax.fori_loop(0, SEGS * ROWS // BLOCK_ROWS, one, 0)

    def place(s, carry):
        ry, rz = relative_patch(place_ref, owner_ref[0, s])
        rows = pl.ds(offset_ref[0, s], ROWS)
        weight = weight_ref[0, s]
        of = pl.ds(pl.multiple_of(s * ROWS, ROWS), ROWS)
        for block in range(BLOCKS):
            sums[block, ry, rz, rows, :] += weight * lifted[block, of, :]
        return carry

    lax.fori_loop(0, SEGS, place, 0, unroll=2)
    write_out(place_ref, sums, (keep_x, send_x, keep_y, send_y), sems)


SMEM = pl.BlockSpec(memory_space=pltpu.SMEM)
VMEM = pl.BlockSpec(memory_space=pltpu.VMEM)
ANY = pl.BlockSpec(memory_space=pl.ANY)
PARTS_X = jax.ShapeDtypeStruct((NX, 2, NY, NZ, 8, LANES), F32)
PARTS_Y = jax.ShapeDtypeStruct((NY, NX, 2, NZ, 8, LANES), F32)
PARAMS = pltpu.CompilerParams(vmem_limit_bytes=40 * 1024 * 1024)
SUMS = pltpu.VMEM((BLOCKS, NY, NZ, 64, LANES), F32)


def denom_sums(place, owner, offset, weight, row_frac, bits, col_base, col_frac):
    return pl.pallas_call(
        denom_kernel,
        out_shape=(PARTS_X, PARTS_X, PARTS_Y, PARTS_Y),
        in_specs=[SMEM] * 5 + [VMEM] * 3,
        out_specs=(ANY,) * 4,
        scratch_shapes=[SUMS, pltpu.VMEM((BLOCKS, SEGS, LANES), F32), pltpu.SemaphoreType.DMA((32,))],
        compiler_params=PARAMS,
        cost_estimate=pl.CostEstimate(flops=10**8, bytes_accessed=4 * 10**6, transcendentals=0),
        name="denom_sums",
    )(place, owner, offset, weight, row_frac, bits, col_base, col_frac)


def row_pass(bank, index, coeff, row_base, row_frac, bits, pixels):
    wide = jax.ShapeDtypeStruct((SEGS * ROWS, NBASIS * WIDTH), BF16)
    return pl.pallas_call(
        rows_kernel,
        out_shape=(wide, wide),
        in_specs=[SMEM] * 5 + [VMEM] * 2,
        out_specs=(VMEM, VMEM),
        scratch_shapes=[pltpu.VMEM((NBASIS * BLOCK_ROWS, 3 * BLOCK_ROWS), BF16)],
        compiler_params=PARAMS,
        cost_estimate=pl.CostEstimate(flops=5 * 10**9, bytes_accessed=8 * 10**6, transcendentals=0),
        name="row_pass",
    )(bank, index, coeff, row_base, row_frac, bits, pixels)


def numer_sums(place, owner, offset, weight, bank, index, col_base, col_frac, u_high, u_low):
    band = pltpu.VMEM((NBASIS * WIDTH, WIDTH), BF16)
    warp = pltpu.VMEM((WIDTH, WIDTH), BF16)
    return pl.pallas_call(
        numer_kernel,
        out_shape=(PARTS_X, PARTS_X, PARTS_Y, PARTS_Y),
        in_specs=[SMEM] * 6 + [VMEM] * 4,
        out_specs=(ANY,) * 4,
        scratch_shapes=[
            SUMS, pltpu.VMEM((BLOCKS, SEGS * ROWS, LANES), F32), band, band, warp, warp,
            pltpu.SemaphoreType.DMA((32,)),
        ],
        compiler_params=PARAMS,
        cost_estimate=pl.CostEstimate(flops=10**10, bytes_accessed=10**7, transcendentals=0),
        name="numer_sums",
    )(place, owner, offset, weight, bank, index, col_base, col_frac, u_high, u_low)


def shift_core(value):
    return lax.ppermute(value, "grp", [(i, i ^ 1) for i in range(2 * NX)])


def shift_x(value, d):
    return lax.ppermute(value, "grp", [(i, (i // 2 + d) % NX * 2 + i % 2) for i in range(2 * NX)])


def shift_y(value, d):
    return lax.ppermute(value, "sky", [(i, i // NY * NY + (i + d) % NY) for i in range(NY * NZ)])


def shift_z(value, d):
    return lax.ppermute(value, "sky", [(i, (i // NY + d) % NZ * NY + i % NY) for i in range(NY * NZ)])


def exchange(parts, shift):
    return [parts[0]] + [shift(parts[d], d) for d in range(1, len(parts))]


def total(terms, take):
    result = take(terms[0])
    for term in terms[1:]:
        result = result + take(term)
    return result


def travel(keep_x, send_x, keep_y, send_y):
    own_x = [keep_x, shift_core(send_x)]
    own_y = [keep_y, shift_core(send_y)]
    by_x = exchange([total(own_x, lambda t: t[d]) for d in range(NX)], shift_x)
    by_y = exchange([total(own_y, lambda t: t[d]) for d in range(NY)], shift_y)
    by_xy = exchange([total(by_x, lambda t: t[:, d]) for d in range(NY)], shift_y)
    by_yx = exchange([total(by_y, lambda t: t[d]) for d in range(NX)], shift_x)
    last = exchange(
        [
            jnp.concatenate([total(by_xy, lambda t: t[:, d]), total(by_yx, lambda t: t[:, d])])
            for d in range(NZ)
        ],
        shift_z,
    )
    return total(last, lambda t: t)


def per_device(
    pixels, mask_bits, owner, row_offset, seg_weight, psf_bank, basis_index, basis_coeff,
    row_base, row_frac, col_base, col_frac,
):
    sky = lax.axis_index("sky").astype(jnp.int32)
    grp = lax.axis_index("grp").astype(jnp.int32)
    place = jnp.stack([grp % 2, grp // 2, sky % NY, sky // NY])
    denom_parts = denom_sums(place, owner, row_offset, seg_weight, row_frac, mask_bits, col_base, col_frac)
    u_high, u_low = row_pass(psf_bank, basis_index, basis_coeff, row_base, row_frac, mask_bits, pixels)
    numer_parts = numer_sums(
        place, owner, row_offset, seg_weight, psf_bank, basis_index, col_base, col_frac, u_high, u_low
    )
    denom = travel(*denom_parts)
    numer = travel(*numer_parts)
    coadd = numer / jnp.maximum(denom, 1.0)
    return jnp.swapaxes(coadd, 0, 1).reshape(8, WIDTH)


def solution(mesh):
    placed = (
        P("grp", "sky", None, None),
        P("grp", "sky", None),
        P("grp", "sky"),
        P("grp", "sky"),
        P("grp", "sky"),
        P(),
        P("grp", None),
        P("grp", None),
        P("grp", None),
        P("grp", None),
        P("grp", None),
        P("grp", None),
    )
    return jax.shard_map(
        per_device, mesh=mesh, in_specs=placed, out_specs=P(("sky", "grp"), None), check_vma=False
    )
```

```python
import functools

import jax
import jax.numpy as jnp
from jax import lax
from jax.experimental import pallas as pl
from jax.experimental.pallas import tpu as pltpu
from jax.sharding import PartitionSpec as P

F32 = jnp.float32
BF16 = jnp.bfloat16
NX, NY, NZ = 4, 4, 8
SEGS = 64
ROWS = 16
WIDTH = 512
TAPS = 21
REACH = 10
NBASIS = 3
LANES = 128
BLOCKS = WIDTH // LANES
BLOCK_SEGS = 16
BLOCK_ROWS = BLOCK_SEGS * ROWS


def split(value):
    high = value.astype(BF16)
    return high, (value - high.astype(F32)).astype(BF16)


def column_factor(bits):
    bad = (bits & 1).astype(F32)
    full = ((bits >> 1) & 1).astype(F32)
    cosmic = ((bits >> 2) & 1).astype(F32)
    return (1.0 - bad) * (1.0 - 0.75 * full) * (1.0 - 0.5 * cosmic)


def column_warp(base, frac):
    source = lax.broadcasted_iota(jnp.int32, (WIDTH, base.shape[1]), 0)
    return jnp.where(source == base, 1.0 - frac, 0.0) + jnp.where(source == base + 1, frac, 0.0)


def column_of(ref, shape):
    row = lax.broadcasted_iota(jnp.int32, shape, 0)
    result = jnp.full(shape, ref[0, 0])
    for i in range(1, ROWS):
        result = jnp.where(row == i, ref[0, i], result)
    return result


A_FIRST = (0, 3, 1, 2)
B_FIRST = (0, 1, 3, 2)


def relative_patch(place_ref, owner):
    ry = (owner % NY) ^ place_ref[2]
    rz = (owner // NY) ^ place_ref[3]
    return ry, (rz & 1) * 4 + ((rz >> 1) ^ (rz >> 2)) % 2 * 2 + (rz >> 2)


def write_out(place_ref, source, keep, send, sems, order):
    copies = []
    for to, core in ((keep, place_ref[0]), (send, 1 - place_ref[0])):
        for pu, ru in enumerate(order):
            for pv, rv in enumerate(A_FIRST):
                rx = ru + core * (rv - ru)
                ry = rv + core * (ru - rv)
                rows = pl.ds(pl.multiple_of((place_ref[1] ^ rx) * 16, 16), 16)
                copies.append((source(core, ry, rows), to.at[pu, pv]))
    started = [pltpu.make_async_copy(src, dst, sems.at[i]) for i, (src, dst) in enumerate(copies)]
    for copy in started:
        copy.start()
    for copy in started:
        copy.wait()


def denom_kernel(
    place_hbm, owner_hbm, offset_hbm, weight_hbm, frac_hbm, bits_ref, col_base_ref, col_frac_ref,
    keep, send, place_ref, owner_ref, offset_ref, weight_ref, frac_ref, sums, cover, sems,
):
    small = [
        pltpu.make_async_copy(src, dst, sems.at[i])
        for i, (src, dst) in enumerate(
            (
                (place_hbm, place_ref), (owner_hbm, owner_ref), (offset_hbm, offset_ref),
                (weight_hbm, weight_ref), (frac_hbm, frac_ref),
            )
        )
    ]
    for copy in small:
        copy.start()
    factor = column_factor(bits_ref[0]).astype(BF16)
    warp_high, warp_low = split(column_warp(col_base_ref[...], col_frac_ref[...]))
    coverage = jnp.dot(factor, warp_high, preferred_element_type=F32) + jnp.dot(
        factor, warp_low, preferred_element_type=F32
    )
    for block in range(BLOCKS):
        cover[block // 2, block % 2] = coverage[:, block * LANES : (block + 1) * LANES]
    sums[...] = jnp.zeros(sums.shape, F32)
    for copy in small:
        copy.wait()
    frac = column_of(frac_ref, (ROWS, LANES))
    spread = (1.0 - frac) + frac

    def one(s, carry):
        ry, rz = relative_patch(place_ref, owner_ref[0, s])
        rows = pl.ds(offset_ref[0, s], ROWS)
        share = spread * weight_ref[0, s]
        for half in range(2):
            for j in range(2):
                sums[half, j, ry, rz, rows, :] += share * cover[half, j, pl.ds(s, 1), :]
        return carry

    lax.fori_loop(0, SEGS, one, 0, unroll=2)
    write_out(place_ref, lambda core, ry, rows: sums.at[core, :, ry, :, rows, :], keep, send, sems, A_FIRST)


def row_tables(bank_ref, index_ref, coeff_ref, base_ref, frac_ref, k):
    shape = (ROWS, BLOCK_ROWS)
    delta = lax.broadcasted_iota(jnp.int32, shape, 1) % ROWS - column_of(base_ref, shape) + REACH
    frac = column_of(frac_ref, shape)
    term = index_ref[0, k]
    lower = jnp.zeros(shape, F32)
    higher = jnp.zeros(shape, F32)
    for tap in range(TAPS):
        value = bank_ref[term, 0, tap]
        lower = jnp.where(delta == tap, value, lower)
        higher = jnp.where(delta == tap + 1, value, higher)
    return ((1.0 - frac) * lower + frac * higher) * coeff_ref[0, k]


def band_tables(bank_ref, index_ref, k):
    lane = lax.broadcasted_iota(jnp.int32, (LANES, WIDTH), 1)
    term = index_ref[0, k]
    base = jnp.zeros((LANES, WIDTH), F32)
    for tap in range(TAPS):
        base = jnp.where(lane == LANES + REACH - tap, bank_ref[term, 1, tap], base)
    return pltpu.roll(base, 0, 1, stride=1, stride_axis=0)[:, : 3 * LANES]


def rows_kernel(
    bank_ref, index_ref, coeff_ref, base_ref, frac_ref, bits_ref, pixels_ref, after, u_high, u_low, blockdiag
):
    same = (
        lax.broadcasted_iota(jnp.int32, (BLOCK_ROWS, BLOCK_ROWS), 0) // ROWS
        == lax.broadcasted_iota(jnp.int32, (BLOCK_ROWS, BLOCK_ROWS), 1) // ROWS
    )
    for k in range(NBASIS):
        table = row_tables(bank_ref, index_ref, coeff_ref, base_ref, frac_ref, k)
        whole = jnp.where(same, jnp.concatenate([table] * BLOCK_SEGS, axis=0), 0.0)
        high, low = split(whole)
        rows = slice(k * BLOCK_ROWS, (k + 1) * BLOCK_ROWS)
        blockdiag[rows, 0:BLOCK_ROWS] = high
        blockdiag[rows, BLOCK_ROWS : 2 * BLOCK_ROWS] = high
        blockdiag[rows, 2 * BLOCK_ROWS :] = low

    def one(b, carry):
        segs = pl.ds(b * BLOCK_SEGS, BLOCK_SEGS)
        factor = column_factor(bits_ref[0, segs, :])
        masked = (pixels_ref[0, segs] * factor[:, None, :]).reshape(BLOCK_ROWS, WIDTH)
        high, low = split(masked)
        product = jnp.dot(
            blockdiag[...], jnp.concatenate([high, low, high], axis=0), preferred_element_type=F32
        )
        rows = pl.ds(pl.multiple_of(b * BLOCK_ROWS, BLOCK_ROWS), BLOCK_ROWS)
        for k in range(NBASIS):
            part_high, part_low = split(product[k * BLOCK_ROWS : (k + 1) * BLOCK_ROWS])
            u_high[rows, k * WIDTH : (k + 1) * WIDTH] = part_high
            u_low[rows, k * WIDTH : (k + 1) * WIDTH] = part_low
        return carry

    lax.fori_loop(0, SEGS // BLOCK_SEGS, one, 0)


def band_kernel(bank_ref, index_ref, u_high, u_low, after, high_ref, low_ref, band_high, band_low):
    band_high[...] = jnp.zeros(band_high.shape, BF16)
    band_low[...] = jnp.zeros(band_low.shape, BF16)
    for k in range(NBASIS):
        high, low = split(band_tables(bank_ref, index_ref, k))
        for block in range(BLOCKS):
            first = max(block - 1, 0)
            last = min(block + 1, BLOCKS - 1)
            rows = slice(k * WIDTH + block * LANES, k * WIDTH + (block + 1) * LANES)
            to = slice(first * LANES, (last + 1) * LANES)
            of = slice((first - block + 1) * LANES, (last - block + 2) * LANES)
            band_high[rows, to] = high[:, of]
            band_low[rows, to] = low[:, of]
    dot = functools.partial(jnp.dot, preferred_element_type=F32)

    def one(b, carry):
        rows = pl.ds(pl.multiple_of(b * BLOCK_ROWS, BLOCK_ROWS), BLOCK_ROWS)
        part_high = u_high[rows, :]
        part_low = u_low[rows, :]
        wide = dot(part_high, band_high[...]) + dot(part_high, band_low[...]) + dot(part_low, band_high[...])
        high, low = split(wide)
        high_ref[rows, :] = high
        low_ref[rows, :] = low
        return carry

    lax.fori_loop(0, SEGS * ROWS // BLOCK_ROWS, one, 0)


def place_kernel(
    chunk, place_ref, owner_ref, offset_ref, weight_ref, col_base_ref, col_frac_ref, high_ref, low_ref, after,
    keep, send, sums, lifted, sems,
):
    picked = [slice((2 * half + chunk) * LANES, (2 * half + chunk + 1) * LANES) for half in range(2)]
    base = jnp.concatenate([col_base_ref[:, cols] for cols in picked], axis=1)
    frac = jnp.concatenate([col_frac_ref[:, cols] for cols in picked], axis=1)
    warp_high, warp_low = split(column_warp(base, frac))
    dot = functools.partial(jnp.dot, preferred_element_type=F32)
    high = high_ref[...]
    warped = dot(high, warp_high) + dot(high, warp_low) + dot(low_ref[...], warp_high)
    for half in range(2):
        lifted[half] = warped[:, half * LANES : (half + 1) * LANES]
    sums[...] = jnp.zeros(sums.shape, F32)

    def one(s, carry):
        ry, rz = relative_patch(place_ref, owner_ref[0, s])
        rows = pl.ds(offset_ref[0, s], ROWS)
        weight = weight_ref[0, s]
        of = pl.ds(pl.multiple_of(s * ROWS, ROWS), ROWS)
        for half in range(2):
            sums[half, ry, rz, rows, :] += weight * lifted[half, of, :]
        return carry

    lax.fori_loop(0, SEGS, one, 0, unroll=2)
    order = (A_FIRST, B_FIRST)[chunk]
    write_out(place_ref, lambda core, ry, rows: sums.at[core, ry, :, rows, :], keep, send, sems, order)


SMEM = pl.BlockSpec(memory_space=pltpu.SMEM)
VMEM = pl.BlockSpec(memory_space=pltpu.VMEM)
ANY = pl.BlockSpec(memory_space=pl.ANY)
PARAMS = pltpu.CompilerParams(vmem_limit_bytes=40 * 1024 * 1024)


def denom_sums(place, owner, offset, weight, row_frac, bits, col_base, col_frac):
    parts = jax.ShapeDtypeStruct((4, 4, 2, NZ, 16, LANES), F32)
    return pl.pallas_call(
        denom_kernel,
        out_shape=(parts, parts),
        in_specs=[ANY] * 5 + [VMEM] * 3,
        out_specs=(ANY,) * 2,
        scratch_shapes=[
            pltpu.SMEM((4,), jnp.int32), pltpu.SMEM((1, SEGS), jnp.int32), pltpu.SMEM((1, SEGS), jnp.int32),
            pltpu.SMEM((1, SEGS), F32), pltpu.SMEM((1, ROWS), F32),
            pltpu.VMEM((2, 2, NY, NZ, 64, LANES), F32), pltpu.VMEM((2, 2, SEGS, LANES), F32),
            pltpu.SemaphoreType.DMA((32,)),
        ],
        compiler_params=PARAMS,
        cost_estimate=pl.CostEstimate(flops=4 * 10**9, bytes_accessed=4 * 10**6, transcendentals=0),
        name="denom_sums",
    )(place, owner, offset, weight, row_frac, bits, col_base, col_frac)


def row_pass(bank, index, coeff, row_base, row_frac, bits, pixels, after):
    wide = jax.ShapeDtypeStruct((SEGS * ROWS, NBASIS * WIDTH), BF16)
    return pl.pallas_call(
        rows_kernel,
        out_shape=(wide, wide),
        in_specs=[SMEM] * 5 + [VMEM] * 2 + [ANY],
        out_specs=(VMEM, VMEM),
        scratch_shapes=[pltpu.VMEM((NBASIS * BLOCK_ROWS, 3 * BLOCK_ROWS), BF16)],
        compiler_params=PARAMS,
        cost_estimate=pl.CostEstimate(flops=4 * 10**9, bytes_accessed=8 * 10**6, transcendentals=0),
        name="row_pass",
    )(bank, index, coeff, row_base, row_frac, bits, pixels, after)


def band_pass(bank, index, u_high, u_low, after):
    wide = jax.ShapeDtypeStruct((SEGS * ROWS, WIDTH), BF16)
    band = pltpu.VMEM((NBASIS * WIDTH, WIDTH), BF16)
    return pl.pallas_call(
        band_kernel,
        out_shape=(wide, wide),
        in_specs=[SMEM] * 2 + [VMEM] * 2 + [ANY],
        out_specs=(VMEM, VMEM),
        scratch_shapes=[band, band],
        compiler_params=PARAMS,
        cost_estimate=pl.CostEstimate(flops=6 * 10**9, bytes_accessed=8 * 10**6, transcendentals=0),
        name="band_pass",
    )(bank, index, u_high, u_low, after)


def numer_sums(chunk, place, owner, offset, weight, col_base, col_frac, high, low, after):
    parts = jax.ShapeDtypeStruct((4, 4, NZ, 16, LANES), F32)
    return pl.pallas_call(
        functools.partial(place_kernel, chunk),
        out_shape=(parts, parts),
        in_specs=[SMEM] * 4 + [VMEM] * 4 + [ANY],
        out_specs=(ANY,) * 2,
        scratch_shapes=[
            pltpu.VMEM((2, NY, NZ, 64, LANES), F32), pltpu.VMEM((2, SEGS * ROWS, LANES), F32),
            pltpu.SemaphoreType.DMA((32,)),
        ],
        compiler_params=PARAMS,
        cost_estimate=pl.CostEstimate(flops=3 * 10**9, bytes_accessed=4 * 10**6, transcendentals=0),
        name=f"numer_sums_{chunk}",
    )(place, owner, offset, weight, col_base, col_frac, high, low, after)


def permute(value, partner):
    pairs = []
    for z in range(NZ):
        for y in range(NY):
            for x in range(NX):
                for core in range(2):
                    to_core, to_x, to_y, to_z = partner(core, x, y, z)
                    source = (z * NY + y) * 2 * NX + x * 2 + core
                    pairs.append((source, (to_z * NY + to_y) * 2 * NX + to_x * 2 + to_core))
    return lax.ppermute(value, ("sky", "grp"), pairs)


def swap_core(value):
    return permute(value, lambda core, x, y, z: (1 - core, x, y, z))


def swap_u(value, step):
    return permute(value, lambda core, x, y, z: (core, x, y ^ step, z) if core else (core, x ^ step, y, z))


def swap_v(value, step):
    return permute(value, lambda core, x, y, z: (core, x ^ step, y, z) if core else (core, x, y ^ step, z))


def swap_z(value, step):
    return permute(value, lambda core, x, y, z: (core, x, y, z ^ step))


def halve(keep, got):
    middle = keep.shape[0] // 2
    return keep[:middle] + got[:middle], keep[middle:] + got[middle:]


def per_device(
    pixels, mask_bits, owner, row_offset, seg_weight, psf_bank, basis_index, basis_coeff,
    row_base, row_frac, col_base, col_frac,
):
    sky = lax.axis_index("sky").astype(jnp.int32)
    grp = lax.axis_index("grp").astype(jnp.int32)
    place = jnp.stack([grp % 2, grp // 2, sky % NY, sky // NY])
    d_keep, d_send = denom_sums(place, owner, row_offset, seg_weight, row_frac, mask_bits, col_base, col_frac)
    u_high, u_low = row_pass(psf_bank, basis_index, basis_coeff, row_base, row_frac, mask_bits, pixels, d_send)
    d_keep, d_send = halve(d_keep, swap_core(d_send))
    high, low = band_pass(psf_bank, basis_index, u_high, u_low, d_send)
    d_got = swap_u(d_send, 1)
    first = numer_sums(0, place, owner, row_offset, seg_weight, col_base, col_frac, high, low, high)
    second = numer_sums(1, place, owner, row_offset, seg_weight, col_base, col_frac, high, low, first[1])
    n_parts = [halve(keep, swap_core(send)) for keep, send in (first, second)]
    d_keep, d_send = halve(d_keep, d_got)
    d_got = swap_u(d_send, 3)
    n_parts = [halve(keep, swap_u(send, step)) for (keep, send), step in zip(n_parts, (1, 3))]
    n_parts = [keep[0] + swap_u(send, step)[0] for (keep, send), step in zip(n_parts, (3, 1))]
    d_part = (d_keep + d_got)[0]
    both = jnp.concatenate([jnp.stack(n_parts, axis=1), d_part], axis=1)
    keep, send = halve(both[:2], swap_v(both[2:], 1))
    both = jnp.swapaxes((keep + swap_v(send, 3))[0], 0, 1)
    keep, send = halve(both[:4], swap_z(both[4:], 1))
    keep, send = halve(keep, swap_z(send, 2))
    both = (keep + swap_z(send, 6))[0]
    coadd = both[:2] / jnp.maximum(both[2:], 1.0)
    coadd = jnp.swapaxes(coadd.reshape(2, 2, 8, LANES), 0, 1)
    odd = place[0] == 1
    mine = jnp.where(odd, coadd[1], coadd[0])
    other = swap_core(jnp.where(odd, coadd[0], coadd[1]))
    blocks = jnp.where(odd, jnp.concatenate([other, mine]), jnp.concatenate([mine, other]))
    return jnp.swapaxes(blocks, 0, 1).reshape(8, WIDTH)


def solution(mesh):
    placed = (
        P("grp", "sky", None, None),
        P("grp", "sky", None),
        P("grp", "sky"),
        P("grp", "sky"),
        P("grp", "sky"),
        P(),
        P("grp", None),
        P("grp", None),
        P("grp", None),
        P("grp", None),
        P("grp", None),
        P("grp", None),
    )
    return jax.shard_map(
        per_device, mesh=mesh, in_specs=placed, out_specs=P(("sky", "grp"), None), check_vma=False
    )
```

```python
import functools

import jax
import jax.numpy as jnp
from jax import lax
from jax.experimental import pallas as pl
from jax.experimental.pallas import tpu as pltpu
from jax.sharding import PartitionSpec as P

F32 = jnp.float32
BF16 = jnp.bfloat16
NX, NY, NZ = 4, 4, 8
SEGS = 64
ROWS = 16
WIDTH = 512
TAPS = 21
REACH = 10
NBASIS = 3
LANES = 128
BLOCKS = WIDTH // LANES
BLOCK_SEGS = 16
BLOCK_ROWS = BLOCK_SEGS * ROWS
OWNER = 4
OFFSET = OWNER + SEGS
INDEX = OFFSET + SEGS
ROW_BASE = INDEX + NBASIS
FRAC = SEGS
COEFF = FRAC + ROWS
BANK = COEFF + NBASIS


def split(value):
    high = value.astype(BF16)
    return high, (value - high.astype(F32)).astype(BF16)


def column_factor(bits):
    bad = (bits & 1).astype(F32)
    full = ((bits >> 1) & 1).astype(F32)
    cosmic = ((bits >> 2) & 1).astype(F32)
    return (1.0 - bad) * (1.0 - 0.75 * full) * (1.0 - 0.5 * cosmic)


def column_warp(base, frac):
    source = lax.broadcasted_iota(jnp.int32, (WIDTH, base.shape[1]), 0).astype(F32)
    return jnp.where(source == base, 1.0 - frac, 0.0) + jnp.where(source == base + 1, frac, 0.0)


def column_of(ref, start, shape):
    row = lax.broadcasted_iota(jnp.int32, shape, 0)
    result = jnp.full(shape, ref[start])
    for i in range(1, ROWS):
        result = jnp.where(row == i, ref[start + i], result)
    return result


A_FIRST = (0, 3, 1, 2)
B_FIRST = (0, 1, 3, 2)


def relative_patch(ints, owner):
    ry = (owner % NY) ^ ints[2]
    rz = (owner // NY) ^ ints[3]
    return ry, (rz & 1) * 4 + ((rz >> 1) ^ (rz >> 2)) % 2 * 2 + (rz >> 2)


def write_out(ints, sums, keep, send, sems, u_order, v_order):
    copies = []
    for to, core in ((keep, ints[0]), (send, 1 - ints[0])):
        for pu, ru in enumerate(u_order):
            for pv, rv in enumerate(v_order):
                rx = ru + core * (rv - ru)
                ry = rv + core * (ru - rv)
                rows = pl.ds(pl.multiple_of(((ints[1] ^ rx) * 2 + core) * 8, 8), 8)
                copies.append((sums.at[:, ry, :, rows, :], to.at[pu, pv]))
    started = [pltpu.make_async_copy(src, dst, sems.at[i]) for i, (src, dst) in enumerate(copies)]
    for copy in started:
        copy.start()
    for copy in started:
        copy.wait()


def denom_kernel(ints, floats, bits_ref, columns_ref, keep, send, sums, cover, sems):
    factor = column_factor(bits_ref[0]).astype(BF16)
    warp_high, warp_low = split(column_warp(columns_ref[0:1, :], columns_ref[1:2, :]))
    coverage = jnp.dot(factor, warp_high, preferred_element_type=F32) + jnp.dot(
        factor, warp_low, preferred_element_type=F32
    )
    for block in range(BLOCKS):
        cover[block] = coverage[:, block * LANES : (block + 1) * LANES]
    sums[...] = jnp.zeros(sums.shape, F32)
    frac = column_of(floats, FRAC, (ROWS, LANES))
    spread = (1.0 - frac) + frac

    def one(s, carry):
        ry, rz = relative_patch(ints, ints[OWNER + s])
        rows = pl.ds(ints[OFFSET + s], ROWS)
        share = spread * floats[s]
        for block in range(BLOCKS):
            sums[block, ry, rz, rows, :] += share * cover[block, pl.ds(s, 1), :]
        return carry

    lax.fori_loop(0, SEGS, one, 0, unroll=2)
    write_out(ints, sums, keep, send, sems, A_FIRST, A_FIRST)


def row_tables(ints, floats, k):
    shape = (ROWS, BLOCK_ROWS)
    delta = lax.broadcasted_iota(jnp.int32, shape, 1) % ROWS - column_of(ints, ROW_BASE, shape) + REACH
    frac = column_of(floats, FRAC, shape)
    term = ints[INDEX + k]
    lower = jnp.zeros(shape, F32)
    higher = jnp.zeros(shape, F32)
    for tap in range(TAPS):
        value = floats[BANK + (2 * term) * TAPS + tap]
        lower = jnp.where(delta == tap, value, lower)
        higher = jnp.where(delta == tap + 1, value, higher)
    return ((1.0 - frac) * lower + frac * higher) * floats[COEFF + k]


def band_tables(ints, floats, k):
    lane = lax.broadcasted_iota(jnp.int32, (LANES, WIDTH), 1)
    term = ints[INDEX + k]
    base = jnp.zeros((LANES, WIDTH), F32)
    for tap in range(TAPS):
        base = jnp.where(lane == LANES + REACH - tap, floats[BANK + (2 * term + 1) * TAPS + tap], base)
    return pltpu.roll(base, 0, 1, stride=1, stride_axis=0)[:, : 3 * LANES]


def rows_kernel(ints, floats, bits_ref, pixels_ref, after, u_high, u_low, blockdiag):
    same = (
        lax.broadcasted_iota(jnp.int32, (BLOCK_ROWS, BLOCK_ROWS), 0) // ROWS
        == lax.broadcasted_iota(jnp.int32, (BLOCK_ROWS, BLOCK_ROWS), 1) // ROWS
    )
    for k in range(NBASIS):
        table = row_tables(ints, floats, k)
        whole = jnp.where(same, jnp.concatenate([table] * BLOCK_SEGS, axis=0), 0.0)
        high, low = split(whole)
        rows = slice(k * BLOCK_ROWS, (k + 1) * BLOCK_ROWS)
        blockdiag[rows, 0:BLOCK_ROWS] = high
        blockdiag[rows, BLOCK_ROWS : 2 * BLOCK_ROWS] = high
        blockdiag[rows, 2 * BLOCK_ROWS :] = low

    def one(b, carry):
        segs = pl.ds(b * BLOCK_SEGS, BLOCK_SEGS)
        factor = column_factor(bits_ref[0, segs, :])
        masked = (pixels_ref[0, segs] * factor[:, None, :]).reshape(BLOCK_ROWS, WIDTH)
        high, low = split(masked)
        product = jnp.dot(
            blockdiag[...], jnp.concatenate([high, low, high], axis=0), preferred_element_type=F32
        )
        rows = pl.ds(pl.multiple_of(b * BLOCK_ROWS, BLOCK_ROWS), BLOCK_ROWS)
        for k in range(NBASIS):
            part_high, part_low = split(product[k * BLOCK_ROWS : (k + 1) * BLOCK_ROWS])
            u_high[rows, k * WIDTH : (k + 1) * WIDTH] = part_high
            u_low[rows, k * WIDTH : (k + 1) * WIDTH] = part_low
        return carry

    lax.fori_loop(0, SEGS // BLOCK_SEGS, one, 0)


def band_kernel(ints, floats, u_high, u_low, after, high_ref, low_ref, band_high, band_low):
    band_high[...] = jnp.zeros(band_high.shape, BF16)
    band_low[...] = jnp.zeros(band_low.shape, BF16)
    for k in range(NBASIS):
        high, low = split(band_tables(ints, floats, k))
        for block in range(BLOCKS):
            first = max(block - 1, 0)
            last = min(block + 1, BLOCKS - 1)
            rows = slice(k * WIDTH + block * LANES, k * WIDTH + (block + 1) * LANES)
            to = slice(first * LANES, (last + 1) * LANES)
            of = slice((first - block + 1) * LANES, (last - block + 2) * LANES)
            band_high[rows, to] = high[:, of]
            band_low[rows, to] = low[:, of]
    dot = functools.partial(jnp.dot, preferred_element_type=F32)

    def one(b, carry):
        rows = pl.ds(pl.multiple_of(b * BLOCK_ROWS, BLOCK_ROWS), BLOCK_ROWS)
        part_high = u_high[rows, :]
        part_low = u_low[rows, :]
        wide = dot(part_high, band_high[...]) + dot(part_high, band_low[...]) + dot(part_low, band_high[...])
        high, low = split(wide)
        high_ref[rows, :] = high
        low_ref[rows, :] = low
        return carry

    lax.fori_loop(0, SEGS * ROWS // BLOCK_ROWS, one, 0)


def place_kernel(
    chunk, ints, floats, columns_ref, high_ref, low_ref, after, keep, send, sums, lifted, sems
):
    cols = slice(2 * chunk * LANES, 2 * (chunk + 1) * LANES)
    warp_high, warp_low = split(column_warp(columns_ref[0:1, cols], columns_ref[1:2, cols]))
    dot = functools.partial(jnp.dot, preferred_element_type=F32)
    high = high_ref[...]
    warped = dot(high, warp_high) + dot(high, warp_low) + dot(low_ref[...], warp_high)
    for half in range(2):
        lifted[half] = warped[:, half * LANES : (half + 1) * LANES]
    sums[...] = jnp.zeros(sums.shape, F32)

    def one(s, carry):
        ry, rz = relative_patch(ints, ints[OWNER + s])
        rows = pl.ds(ints[OFFSET + s], ROWS)
        weight = floats[s]
        of = pl.ds(pl.multiple_of(s * ROWS, ROWS), ROWS)
        for half in range(2):
            sums[half, ry, rz, rows, :] += weight * lifted[half, of, :]
        return carry

    lax.fori_loop(0, SEGS, one, 0, unroll=2)
    order = (A_FIRST, B_FIRST)[chunk]
    write_out(ints, sums, keep, send, sems, order, B_FIRST)


SMEM = pl.BlockSpec(memory_space=pltpu.SMEM)
VMEM = pl.BlockSpec(memory_space=pltpu.VMEM)
ANY = pl.BlockSpec(memory_space=pl.ANY)
PARAMS = pltpu.CompilerParams(vmem_limit_bytes=40 * 1024 * 1024)


def denom_sums(ints, floats, bits, columns):
    parts = jax.ShapeDtypeStruct((4, 4, BLOCKS, NZ, 8, LANES), F32)
    return pl.pallas_call(
        denom_kernel,
        out_shape=(parts, parts),
        in_specs=[SMEM] * 2 + [VMEM] * 2,
        out_specs=(ANY,) * 2,
        scratch_shapes=[
            pltpu.VMEM((BLOCKS, NY, NZ, 64, LANES), F32), pltpu.VMEM((BLOCKS, SEGS, LANES), F32),
            pltpu.SemaphoreType.DMA((32,)),
        ],
        compiler_params=PARAMS,
        cost_estimate=pl.CostEstimate(flops=10**3, bytes_accessed=10**3, transcendentals=0),
        name="denom_sums",
    )(ints, floats, bits, columns)


def row_pass(ints, floats, bits, pixels, after):
    wide = jax.ShapeDtypeStruct((SEGS * ROWS, NBASIS * WIDTH), BF16)
    return pl.pallas_call(
        rows_kernel,
        out_shape=(wide, wide),
        in_specs=[SMEM] * 2 + [VMEM] * 2 + [ANY],
        out_specs=(VMEM, VMEM),
        scratch_shapes=[
            pltpu.VMEM((NBASIS * BLOCK_ROWS, 3 * BLOCK_ROWS), BF16),
        ],
        compiler_params=PARAMS,
        cost_estimate=pl.CostEstimate(flops=10**3, bytes_accessed=10**3, transcendentals=0),
        name="row_pass",
    )(ints, floats, bits, pixels, after)


def band_pass(ints, floats, u_high, u_low, after):
    wide = jax.ShapeDtypeStruct((SEGS * ROWS, WIDTH), BF16)
    band = pltpu.VMEM((NBASIS * WIDTH, WIDTH), BF16)
    return pl.pallas_call(
        band_kernel,
        out_shape=(wide, wide),
        in_specs=[SMEM] * 2 + [VMEM] * 2 + [ANY],
        out_specs=(VMEM, VMEM),
        scratch_shapes=[band, band],
        compiler_params=PARAMS,
        cost_estimate=pl.CostEstimate(flops=10**3, bytes_accessed=10**3, transcendentals=0),
        name="band_pass",
    )(ints, floats, u_high, u_low, after)


def numer_sums(chunk, ints, floats, columns, high, low, after):
    parts = jax.ShapeDtypeStruct((4, 4, 2, NZ, 8, LANES), F32)
    return pl.pallas_call(
        functools.partial(place_kernel, chunk),
        out_shape=(parts, parts),
        in_specs=[SMEM] * 2 + [VMEM] * 3 + [ANY],
        out_specs=(ANY,) * 2,
        scratch_shapes=[
            pltpu.VMEM((2, NY, NZ, 64, LANES), F32), pltpu.VMEM((2, SEGS * ROWS, LANES), F32),
            pltpu.SemaphoreType.DMA((32,)),
        ],
        compiler_params=PARAMS,
        cost_estimate=pl.CostEstimate(flops=10**3, bytes_accessed=10**3, transcendentals=0),
        name=f"numer_sums_{chunk}",
    )(ints, floats, columns, high, low, after)


def permute(value, partner):
    pairs = []
    for z in range(NZ):
        for y in range(NY):
            for x in range(NX):
                for core in range(2):
                    to_core, to_x, to_y, to_z = partner(core, x, y, z)
                    source = (z * NY + y) * 2 * NX + x * 2 + core
                    pairs.append((source, (to_z * NY + to_y) * 2 * NX + to_x * 2 + to_core))
    return lax.ppermute(value, ("sky", "grp"), pairs)


def swap_core(value):
    return permute(value, lambda core, x, y, z: (1 - core, x, y, z))


def swap_u(value, step):
    return permute(value, lambda core, x, y, z: (core, x, y ^ step, z) if core else (core, x ^ step, y, z))


def swap_v(value, step):
    return permute(value, lambda core, x, y, z: (core, x ^ step, y, z) if core else (core, x, y ^ step, z))


def swap_z(value, step):
    return permute(value, lambda core, x, y, z: (core, x, y, z ^ step))


def halve(keep, got):
    middle = keep.shape[0] // 2
    return keep[:middle] + got[:middle], keep[middle:] + got[middle:]


def hold(values, after):
    def kernel(*refs):
        pass

    return pl.pallas_call(
        kernel,
        out_shape=tuple(jax.ShapeDtypeStruct(value.shape, value.dtype) for value in values),
        in_specs=[ANY] * (len(values) + 1),
        out_specs=(ANY,) * len(values),
        input_output_aliases={i: i for i in range(len(values))},
        name="hold",
    )(*values, after)


def per_device(
    pixels, mask_bits, owner, row_offset, seg_weight, psf_bank, basis_index, basis_coeff,
    row_base, row_frac, col_base, col_frac,
):
    sky = lax.axis_index("sky").astype(jnp.int32)
    grp = lax.axis_index("grp").astype(jnp.int32)
    place = jnp.stack([grp % 2, grp // 2, sky % NY, sky // NY])
    ints = jnp.concatenate([place, owner[0], row_offset[0], basis_index[0], row_base[0]])
    floats = jnp.concatenate([seg_weight[0], row_frac[0], basis_coeff[0], psf_bank.reshape(-1)])
    columns = jnp.concatenate([col_base.astype(F32), col_frac])
    d_keep, d_send = denom_sums(ints, floats, mask_bits, columns)
    u_high, u_low = row_pass(ints, floats, mask_bits, pixels, d_send)
    (d_got,) = hold((swap_core(d_send),), u_high)
    d_keep, d_send = halve(d_keep, d_got)
    high, low = band_pass(ints, floats, u_high, u_low, d_send)
    d_got = swap_u(d_send, 1)
    first = numer_sums(0, ints, floats, columns, high, low, high)
    second = numer_sums(1, ints, floats, columns, high, low, first[1])
    d_keep, d_send = halve(d_keep, d_got)
    n_sends = hold((first[1], second[1]), d_send)
    n_got = [swap_core(send) for send in n_sends]
    d_got = swap_u(d_send, 3)
    n_parts = [halve(keep, got) for (keep, _), got in zip((first, second), n_got)]
    n_parts = [halve(keep, swap_u(send, step)) for (keep, send), step in zip(n_parts, (1, 3))]
    d_part = (d_keep + d_got)[0]
    d_keep, d_send = halve(d_part[:2], swap_v(d_part[2:], 1))
    n_parts = [keep[0] + swap_u(send, step)[0] for (keep, send), step in zip(n_parts, (3, 1))]
    n_part = jnp.concatenate(n_parts, axis=1)
    n_keep, n_send = halve(n_part[:2], swap_v(n_part[2:], 3))
    d_part = (d_keep + swap_v(d_send, 3))[0]
    n_part = (n_keep + swap_v(n_send, 1))[0]
    both = jnp.swapaxes(jnp.concatenate([n_part, d_part]), 0, 1)
    keep, send = halve(both[:4], swap_z(both[4:], 1))
    keep, send = halve(keep, swap_z(send, 2))
    both = (keep + swap_z(send, 6))[0]
    coadd = both[:BLOCKS] / jnp.maximum(both[BLOCKS:], 1.0)
    return jnp.swapaxes(coadd, 0, 1).reshape(8, WIDTH)


def solution(mesh):
    placed = (
        P("grp", "sky", None, None),
        P("grp", "sky", None),
        P("grp", "sky"),
        P("grp", "sky"),
        P("grp", "sky"),
        P(),
        P("grp", None),
        P("grp", None),
        P("grp", None),
        P("grp", None),
        P("grp", None),
        P("grp", None),
    )
    return jax.shard_map(
        per_device, mesh=mesh, in_specs=placed, out_specs=P(("sky", "grp"), None), check_vma=False
    )
```

```python
import functools

import jax
import jax.numpy as jnp
from jax import lax
from jax.experimental import pallas as pl
from jax.experimental.pallas import tpu as pltpu
from jax.sharding import PartitionSpec as P

F32 = jnp.float32
BF16 = jnp.bfloat16
NX, NY, NZ = 4, 4, 8
SEGS = 64
ROWS = 16
WIDTH = 512
TAPS = 21
REACH = 10
NBASIS = 3
LANES = 128
BLOCKS = WIDTH // LANES
BLOCK_SEGS = 16
BLOCK_ROWS = BLOCK_SEGS * ROWS


def split(value):
    high = value.astype(BF16)
    return high, (value - high.astype(F32)).astype(BF16)


def column_factor(bits):
    bad = (bits & 1).astype(F32)
    full = ((bits >> 1) & 1).astype(F32)
    cosmic = ((bits >> 2) & 1).astype(F32)
    return (1.0 - bad) * (1.0 - 0.75 * full) * (1.0 - 0.5 * cosmic)


def column_warp(base, frac):
    source = lax.broadcasted_iota(jnp.int32, (WIDTH, base.shape[1]), 0)
    return jnp.where(source == base, 1.0 - frac, 0.0) + jnp.where(source == base + 1, frac, 0.0)


def column_of(ref, shape):
    row = lax.broadcasted_iota(jnp.int32, shape, 0)
    result = jnp.full(shape, ref[0, 0])
    for i in range(1, ROWS):
        result = jnp.where(row == i, ref[0, i], result)
    return result


A_FIRST = (0, 3, 1, 2)
B_FIRST = (0, 1, 3, 2)


def relative_patch(place_ref, owner):
    ry = (owner % NY) ^ place_ref[2]
    rz = (owner // NY) ^ place_ref[3]
    return ry, (rz & 1) * 4 + ((rz >> 1) ^ (rz >> 2)) % 2 * 2 + (rz >> 2)


def write_out(place_ref, sums, keep, send, sems, u_order, v_order):
    copies = []
    for to, core in ((keep, place_ref[0]), (send, 1 - place_ref[0])):
        for pu, ru in enumerate(u_order):
            for pv, rv in enumerate(v_order):
                rx = ru + core * (rv - ru)
                ry = rv + core * (ru - rv)
                rows = pl.ds(pl.multiple_of(((place_ref[1] ^ rx) * 2 + core) * 8, 8), 8)
                copies.append((sums.at[:, ry, :, rows, :], to.at[pu, pv]))
    started = [pltpu.make_async_copy(src, dst, sems.at[i]) for i, (src, dst) in enumerate(copies)]
    for copy in started:
        copy.start()
    for copy in started:
        copy.wait()


def fetch(pairs, sems):
    copies = [pltpu.make_async_copy(src, dst, sems.at[i]) for i, (src, dst) in enumerate(pairs)]
    for copy in copies:
        copy.start()
    return copies


def denom_kernel(
    place_hbm, owner_hbm, offset_hbm, weight_hbm, frac_hbm, bits_hbm, col_base_hbm, col_frac_hbm,
    keep, send, done, place_ref, owner_ref, offset_ref, weight_ref, frac_ref, bits_ref, col_base_ref, col_frac_ref,
    sums, cover, sems,
):
    small = fetch(
        (
            (place_hbm, place_ref), (owner_hbm, owner_ref), (offset_hbm, offset_ref),
            (weight_hbm, weight_ref), (frac_hbm, frac_ref), (bits_hbm, bits_ref),
            (col_base_hbm, col_base_ref), (col_frac_hbm, col_frac_ref),
        ),
        sems,
    )
    sums[...] = jnp.zeros(sums.shape, F32)
    for copy in small:
        copy.wait()
    factor = column_factor(bits_ref[0]).astype(BF16)
    warp_high, warp_low = split(column_warp(col_base_ref[...], col_frac_ref[...]))
    coverage = jnp.dot(factor, warp_high, preferred_element_type=F32) + jnp.dot(
        factor, warp_low, preferred_element_type=F32
    )
    for block in range(BLOCKS):
        cover[block] = coverage[:, block * LANES : (block + 1) * LANES]
    frac = column_of(frac_ref, (ROWS, LANES))
    spread = (1.0 - frac) + frac

    def one(s, carry):
        ry, rz = relative_patch(place_ref, owner_ref[0, s])
        rows = pl.ds(offset_ref[0, s], ROWS)
        share = spread * weight_ref[0, s]
        for block in range(BLOCKS):
            sums[block, ry, rz, rows, :] += share * cover[block, pl.ds(s, 1), :]
        return carry

    lax.fori_loop(0, SEGS, one, 0, unroll=2)
    write_out(place_ref, sums, keep, send, sems, A_FIRST, A_FIRST)
    done[...] = jnp.zeros(done.shape, F32)


def row_tables(bank_ref, index_ref, coeff_ref, base_ref, frac_ref, k):
    shape = (ROWS, BLOCK_ROWS)
    delta = lax.broadcasted_iota(jnp.int32, shape, 1) % ROWS - column_of(base_ref, shape) + REACH
    frac = column_of(frac_ref, shape)
    term = index_ref[0, k]
    lower = jnp.zeros(shape, F32)
    higher = jnp.zeros(shape, F32)
    for tap in range(TAPS):
        value = bank_ref[term, 0, tap]
        lower = jnp.where(delta == tap, value, lower)
        higher = jnp.where(delta == tap + 1, value, higher)
    return ((1.0 - frac) * lower + frac * higher) * coeff_ref[0, k]


def band_tables(bank_ref, index_ref, k):
    lane = lax.broadcasted_iota(jnp.int32, (LANES, WIDTH), 1)
    term = index_ref[0, k]
    base = jnp.zeros((LANES, WIDTH), F32)
    for tap in range(TAPS):
        base = jnp.where(lane == LANES + REACH - tap, bank_ref[term, 1, tap], base)
    return pltpu.roll(base, 0, 1, stride=1, stride_axis=0)[:, : 3 * LANES]


def rows_kernel(
    bank_hbm, index_hbm, coeff_hbm, base_hbm, frac_hbm, bits_hbm, pixels_hbm, after,
    u_high, u_low, done, bank_ref, index_ref, coeff_ref, base_ref, frac_ref, bits_ref, pixels_ref, blockdiag, sems,
):
    small = fetch(
        (
            (bank_hbm, bank_ref), (index_hbm, index_ref), (coeff_hbm, coeff_ref),
            (base_hbm, base_ref), (frac_hbm, frac_ref), (bits_hbm, bits_ref),
        ),
        sems,
    )
    blocks = SEGS // BLOCK_SEGS

    def fetch_block(b):
        segs = pl.ds(b * BLOCK_SEGS, BLOCK_SEGS)
        return pltpu.make_async_copy(pixels_hbm.at[:, segs], pixels_ref.at[:, segs], sems.at[len(small) + b])

    for b in range(blocks):
        fetch_block(b).start()
    for copy in small:
        copy.wait()
    same = (
        lax.broadcasted_iota(jnp.int32, (BLOCK_ROWS, BLOCK_ROWS), 0) // ROWS
        == lax.broadcasted_iota(jnp.int32, (BLOCK_ROWS, BLOCK_ROWS), 1) // ROWS
    )
    for k in range(NBASIS):
        table = row_tables(bank_ref, index_ref, coeff_ref, base_ref, frac_ref, k)
        whole = jnp.where(same, jnp.concatenate([table] * BLOCK_SEGS, axis=0), 0.0)
        high, low = split(whole)
        rows = slice(k * BLOCK_ROWS, (k + 1) * BLOCK_ROWS)
        blockdiag[rows, 0:BLOCK_ROWS] = high
        blockdiag[rows, BLOCK_ROWS : 2 * BLOCK_ROWS] = high
        blockdiag[rows, 2 * BLOCK_ROWS :] = low

    def one(b, carry):
        fetch_block(b).wait()
        segs = pl.ds(b * BLOCK_SEGS, BLOCK_SEGS)
        factor = column_factor(bits_ref[0, segs, :])
        masked = (pixels_ref[0, segs] * factor[:, None, :]).reshape(BLOCK_ROWS, WIDTH)
        high, low = split(masked)
        product = jnp.dot(
            blockdiag[...], jnp.concatenate([high, low, high], axis=0), preferred_element_type=F32
        )
        rows = pl.ds(pl.multiple_of(b * BLOCK_ROWS, BLOCK_ROWS), BLOCK_ROWS)
        for k in range(NBASIS):
            part_high, part_low = split(product[k * BLOCK_ROWS : (k + 1) * BLOCK_ROWS])
            u_high[rows, k * WIDTH : (k + 1) * WIDTH] = part_high
            u_low[rows, k * WIDTH : (k + 1) * WIDTH] = part_low
        return carry

    lax.fori_loop(0, SEGS // BLOCK_SEGS, one, 0)
    done[...] = jnp.zeros(done.shape, F32)


def band_kernel(
    bank_hbm, index_hbm, u_high, u_low, after, high_ref, low_ref, bank_ref, index_ref, band_high, band_low, sems
):
    small = fetch(((bank_hbm, bank_ref), (index_hbm, index_ref)), sems)
    band_high[...] = jnp.zeros(band_high.shape, BF16)
    band_low[...] = jnp.zeros(band_low.shape, BF16)
    for copy in small:
        copy.wait()
    for k in range(NBASIS):
        high, low = split(band_tables(bank_ref, index_ref, k))
        for block in range(BLOCKS):
            first = max(block - 1, 0)
            last = min(block + 1, BLOCKS - 1)
            rows = slice(k * WIDTH + block * LANES, k * WIDTH + (block + 1) * LANES)
            to = slice(first * LANES, (last + 1) * LANES)
            of = slice((first - block + 1) * LANES, (last - block + 2) * LANES)
            band_high[rows, to] = high[:, of]
            band_low[rows, to] = low[:, of]
    dot = functools.partial(jnp.dot, preferred_element_type=F32)

    def one(b, carry):
        rows = pl.ds(pl.multiple_of(b * BLOCK_ROWS, BLOCK_ROWS), BLOCK_ROWS)
        part_high = u_high[rows, :]
        part_low = u_low[rows, :]
        wide = dot(part_high, band_high[...]) + dot(part_high, band_low[...]) + dot(part_low, band_high[...])
        high, low = split(wide)
        high_ref[rows, :] = high
        low_ref[rows, :] = low
        return carry

    lax.fori_loop(0, SEGS * ROWS // BLOCK_ROWS, one, 0)


def place_kernel(
    chunk, place_ref, owner_ref, offset_ref, weight_ref, col_base_ref, col_frac_ref, high_ref, low_ref, after,
    keep, send, done, sums, lifted, sems,
):
    cols = slice(2 * chunk * LANES, 2 * (chunk + 1) * LANES)
    warp_high, warp_low = split(column_warp(col_base_ref[:, cols], col_frac_ref[:, cols]))
    dot = functools.partial(jnp.dot, preferred_element_type=F32)
    high = high_ref[...]
    warped = dot(high, warp_high) + dot(high, warp_low) + dot(low_ref[...], warp_high)
    for half in range(2):
        lifted[half] = warped[:, half * LANES : (half + 1) * LANES]
    sums[...] = jnp.zeros(sums.shape, F32)

    def one(s, carry):
        ry, rz = relative_patch(place_ref, owner_ref[0, s])
        rows = pl.ds(offset_ref[0, s], ROWS)
        weight = weight_ref[0, s]
        of = pl.ds(pl.multiple_of(s * ROWS, ROWS), ROWS)
        for half in range(2):
            sums[half, ry, rz, rows, :] += weight * lifted[half, of, :]
        return carry

    lax.fori_loop(0, SEGS, one, 0, unroll=2)
    order = (A_FIRST, B_FIRST)[chunk]
    write_out(place_ref, sums, keep, send, sems, order, B_FIRST)
    done[...] = jnp.zeros(done.shape, F32)


SMEM = pl.BlockSpec(memory_space=pltpu.SMEM)
VMEM = pl.BlockSpec(memory_space=pltpu.VMEM)
ANY = pl.BlockSpec(memory_space=pl.ANY)
HBM = pl.BlockSpec(memory_space=pltpu.HBM)
TOKEN = jax.ShapeDtypeStruct((8, LANES), F32)
PARAMS = pltpu.CompilerParams(vmem_limit_bytes=40 * 1024 * 1024)


def pinned(*values):
    return [pltpu.with_memory_space_constraint(value, pltpu.HBM) for value in values]


def denom_sums(place, owner, offset, weight, row_frac, bits, col_base, col_frac):
    parts = jax.ShapeDtypeStruct((4, 4, BLOCKS, NZ, 8, LANES), F32)
    return pl.pallas_call(
        denom_kernel,
        out_shape=(parts, parts, TOKEN),
        in_specs=[HBM] * 8,
        out_specs=(ANY, ANY, VMEM),
        scratch_shapes=[
            pltpu.SMEM((4,), jnp.int32), pltpu.SMEM((1, SEGS), jnp.int32), pltpu.SMEM((1, SEGS), jnp.int32),
            pltpu.SMEM((1, SEGS), F32), pltpu.SMEM((1, ROWS), F32), pltpu.VMEM((1, SEGS, WIDTH), jnp.int32),
            pltpu.VMEM((1, WIDTH), jnp.int32), pltpu.VMEM((1, WIDTH), F32),
            pltpu.VMEM((BLOCKS, NY, NZ, 64, LANES), F32), pltpu.VMEM((BLOCKS, SEGS, LANES), F32),
            pltpu.SemaphoreType.DMA((32,)),
        ],
        compiler_params=PARAMS,
        cost_estimate=pl.CostEstimate(flops=10**3, bytes_accessed=10**3, transcendentals=0),
        name="denom_sums",
    )(*pinned(place, owner, offset, weight, row_frac, bits, col_base, col_frac))


def row_pass(bank, index, coeff, row_base, row_frac, bits, pixels, after):
    wide = jax.ShapeDtypeStruct((SEGS * ROWS, NBASIS * WIDTH), BF16)
    return pl.pallas_call(
        rows_kernel,
        out_shape=(wide, wide, TOKEN),
        in_specs=[HBM] * 7 + [VMEM],
        out_specs=(VMEM, VMEM, VMEM),
        scratch_shapes=[
            pltpu.SMEM(bank.shape, F32), pltpu.SMEM((1, NBASIS), jnp.int32), pltpu.SMEM((1, NBASIS), F32),
            pltpu.SMEM((1, ROWS), jnp.int32), pltpu.SMEM((1, ROWS), F32),
            pltpu.VMEM(bits.shape, jnp.int32), pltpu.VMEM(pixels.shape, F32),
            pltpu.VMEM((NBASIS * BLOCK_ROWS, 3 * BLOCK_ROWS), BF16), pltpu.SemaphoreType.DMA((10,)),
        ],
        compiler_params=PARAMS,
        cost_estimate=pl.CostEstimate(flops=10**3, bytes_accessed=10**3, transcendentals=0),
        name="row_pass",
    )(*pinned(bank, index, coeff, row_base, row_frac, bits, pixels), after)


def band_pass(bank, index, u_high, u_low, after):
    wide = jax.ShapeDtypeStruct((SEGS * ROWS, WIDTH), BF16)
    band = pltpu.VMEM((NBASIS * WIDTH, WIDTH), BF16)
    return pl.pallas_call(
        band_kernel,
        out_shape=(wide, wide),
        in_specs=[HBM] * 2 + [VMEM] * 3,
        out_specs=(VMEM, VMEM),
        scratch_shapes=[
            pltpu.SMEM(bank.shape, F32), pltpu.SMEM(index.shape, jnp.int32), band, band, pltpu.SemaphoreType.DMA((2,))
        ],
        compiler_params=PARAMS,
        cost_estimate=pl.CostEstimate(flops=10**3, bytes_accessed=10**3, transcendentals=0),
        name="band_pass",
    )(*pinned(bank, index), u_high, u_low, after)


def numer_sums(chunk, place, owner, offset, weight, col_base, col_frac, high, low, after):
    parts = jax.ShapeDtypeStruct((4, 4, 2, NZ, 8, LANES), F32)
    return pl.pallas_call(
        functools.partial(place_kernel, chunk),
        out_shape=(parts, parts, TOKEN),
        in_specs=[SMEM] * 4 + [VMEM] * 5,
        out_specs=(ANY, ANY, VMEM),
        scratch_shapes=[
            pltpu.VMEM((2, NY, NZ, 64, LANES), F32), pltpu.VMEM((2, SEGS * ROWS, LANES), F32),
            pltpu.SemaphoreType.DMA((32,)),
        ],
        compiler_params=PARAMS,
        cost_estimate=pl.CostEstimate(flops=10**3, bytes_accessed=10**3, transcendentals=0),
        name=f"numer_sums_{chunk}",
    )(place, owner, offset, weight, col_base, col_frac, high, low, after)


def permute(value, partner):
    pairs = []
    for z in range(NZ):
        for y in range(NY):
            for x in range(NX):
                for core in range(2):
                    to_core, to_x, to_y, to_z = partner(core, x, y, z)
                    source = (z * NY + y) * 2 * NX + x * 2 + core
                    pairs.append((source, (to_z * NY + to_y) * 2 * NX + to_x * 2 + to_core))
    return lax.ppermute(value, ("sky", "grp"), pairs)


def swap_core(value):
    return permute(value, lambda core, x, y, z: (1 - core, x, y, z))


def swap_u(value, step):
    return permute(value, lambda core, x, y, z: (core, x, y ^ step, z) if core else (core, x ^ step, y, z))


def swap_v(value, step):
    return permute(value, lambda core, x, y, z: (core, x ^ step, y, z) if core else (core, x, y ^ step, z))


def swap_z(value, step):
    return permute(value, lambda core, x, y, z: (core, x, y, z ^ step))


def halve(keep, got):
    middle = keep.shape[0] // 2
    return keep[:middle] + got[:middle], keep[middle:] + got[middle:]


def hold(values, after):
    def kernel(*refs):
        pass

    return pl.pallas_call(
        kernel,
        out_shape=tuple(jax.ShapeDtypeStruct(value.shape, value.dtype) for value in values),
        in_specs=[VMEM] * (len(values) + 1),
        out_specs=(VMEM,) * len(values),
        input_output_aliases={i: i for i in range(len(values))},
        compiler_params=PARAMS,
        name="hold",
    )(*values, after)


def per_device(
    pixels, mask_bits, owner, row_offset, seg_weight, psf_bank, basis_index, basis_coeff,
    row_base, row_frac, col_base, col_frac,
):
    sky = lax.axis_index("sky").astype(jnp.int32)
    grp = lax.axis_index("grp").astype(jnp.int32)
    place = jnp.stack([grp % 2, grp // 2, sky % NY, sky // NY])
    d_keep, d_send, done = denom_sums(
        place, owner, row_offset, seg_weight, row_frac, mask_bits, col_base, col_frac
    )
    u_high, u_low, done = row_pass(
        psf_bank, basis_index, basis_coeff, row_base, row_frac, mask_bits, pixels, done
    )
    (d_got,) = hold((swap_core(d_send),), done)
    d_keep, d_send = halve(d_keep, d_got)
    high, low = band_pass(psf_bank, basis_index, u_high, u_low, d_send)
    d_got = swap_u(d_send, 1)
    first = numer_sums(0, place, owner, row_offset, seg_weight, col_base, col_frac, high, low, done)
    second = numer_sums(1, place, owner, row_offset, seg_weight, col_base, col_frac, high, low, first[2])
    d_keep, d_send = halve(d_keep, d_got)
    n_sends = hold((first[1], second[1]), d_send)
    n_got = [swap_core(send) for send in n_sends]
    d_got = swap_u(d_send, 3)
    n_parts = [halve(keep, got) for (keep, _, _), got in zip((first, second), n_got)]
    n_parts = [halve(keep, swap_u(send, step)) for (keep, send), step in zip(n_parts, (1, 3))]
    d_part = (d_keep + d_got)[0]
    d_keep, d_send = halve(d_part[:2], swap_v(d_part[2:], 1))
    n_parts = [keep[0] + swap_u(send, step)[0] for (keep, send), step in zip(n_parts, (3, 1))]
    n_part = jnp.concatenate(n_parts, axis=1)
    n_keep, n_send = halve(n_part[:2], swap_v(n_part[2:], 3))
    d_part = (d_keep + swap_v(d_send, 3))[0]
    n_part = (n_keep + swap_v(n_send, 1))[0]
    both = jnp.swapaxes(jnp.concatenate([n_part, d_part]), 0, 1)
    keep, send = halve(both[:4], swap_z(both[4:], 1))
    keep, send = halve(keep, swap_z(send, 2))
    both = (keep + swap_z(send, 6))[0]
    coadd = both[:BLOCKS] / jnp.maximum(both[BLOCKS:], 1.0)
    return jnp.swapaxes(coadd, 0, 1).reshape(8, WIDTH)


def solution(mesh):
    placed = (
        P("grp", "sky", None, None),
        P("grp", "sky", None),
        P("grp", "sky"),
        P("grp", "sky"),
        P("grp", "sky"),
        P(),
        P("grp", None),
        P("grp", None),
        P("grp", None),
        P("grp", None),
        P("grp", None),
        P("grp", None),
    )
    return jax.shard_map(
        per_device, mesh=mesh, in_specs=placed, out_specs=P(("sky", "grp"), None), check_vma=False
    )
```

```python
import functools

import jax
import jax.numpy as jnp
from jax import lax
from jax.experimental import pallas as pl
from jax.experimental.pallas import tpu as pltpu
from jax.sharding import PartitionSpec as P

F32 = jnp.float32
BF16 = jnp.bfloat16
NX, NY, NZ = 4, 4, 8
SEGS = 64
ROWS = 16
WIDTH = 512
TAPS = 21
REACH = 10
NBASIS = 3
LANES = 128
BLOCKS = WIDTH // LANES
HALF = WIDTH // 2
BLOCK_SEGS = 16
BLOCK_ROWS = BLOCK_SEGS * ROWS


def split(value):
    high = value.astype(BF16)
    return high, (value - high.astype(F32)).astype(BF16)


def column_factor(bits):
    bad = (bits & 1).astype(F32)
    full = ((bits >> 1) & 1).astype(F32)
    cosmic = ((bits >> 2) & 1).astype(F32)
    return (1.0 - bad) * (1.0 - 0.75 * full) * (1.0 - 0.5 * cosmic)


def column_warp(base, frac):
    source = lax.broadcasted_iota(jnp.int32, (WIDTH, base.shape[1]), 0)
    return jnp.where(source == base, 1.0 - frac, 0.0) + jnp.where(source == base + 1, frac, 0.0)


def column_of(ref, shape):
    row = lax.broadcasted_iota(jnp.int32, shape, 0)
    result = jnp.full(shape, ref[0, 0])
    for i in range(1, ROWS):
        result = jnp.where(row == i, ref[0, i], result)
    return result


A_FIRST = (0, 3, 1, 2)
B_FIRST = (0, 1, 3, 2)
U_ORDER = (A_FIRST, B_FIRST)
Z_ORDER = (0, 4, 2, 6, 1, 5, 3, 7)


def own_place():
    sky = lax.axis_index("sky")
    grp = lax.axis_index("grp")
    return grp % 2, grp // 2, sky % NY, sky // NY


def relative_patch(place, owner):
    ry = (owner % NY) ^ place[2]
    rz = (owner // NY) ^ place[3]
    return ry, (rz & 1) * 4 + ((rz >> 1) & 1) * 2 + (rz >> 2)


def write_out(place, sums, keep, send, sems, u_order):
    copies = []
    for to, core in ((keep, place[0]), (send, 1 - place[0])):
        for pu, ru in enumerate(u_order):
            for rv in range(4):
                rx = ru + core * (rv - ru)
                ry = rv + core * (ru - rv)
                rows = pl.ds(pl.multiple_of(((place[1] ^ rx) * 2 + core) * 8, 8), 8)
                copies.append(pltpu.make_async_copy(sums.at[:, ry, :, rows, :], to.at[pu, rv], sems.at[len(copies)]))
    for copy in copies:
        copy.start()
    return copies


def fetch(pairs, sems):
    copies = [pltpu.make_async_copy(src, dst, sems.at[i]) for i, (src, dst) in enumerate(pairs)]
    for copy in copies:
        copy.start()
    return copies


def denom_kernel(
    owner_hbm, offset_hbm, weight_hbm, bank_hbm, index_hbm, coeff_hbm, base_hbm, frac_hbm, bits_hbm,
    col_base_hbm, col_frac_hbm, pixels_hbm,
    keep, send, pixels_ref, factor_ref, blockdiag, profiles, warp_high, warp_low,
    owner_ref, offset_ref, weight_ref, bank_ref, index_ref, coeff_ref, base_ref, frac_ref, bits_ref,
    col_base_ref, col_frac_ref, sums, cover, sems, out_sems,
):
    place = own_place()
    inputs = fetch(
        (
            (owner_hbm, owner_ref), (offset_hbm, offset_ref), (weight_hbm, weight_ref),
            (frac_hbm, frac_ref), (bits_hbm, bits_ref), (col_base_hbm, col_base_ref), (col_frac_hbm, col_frac_ref),
            (bank_hbm, bank_ref), (index_hbm, index_ref), (coeff_hbm, coeff_ref), (base_hbm, base_ref),
            (pixels_hbm, pixels_ref),
        ),
        sems,
    )
    sums[...] = jnp.zeros(sums.shape, F32)
    for copy in inputs[:7]:
        copy.wait()
    factor = column_factor(bits_ref[0])
    factor_ref[...] = factor
    high, low = split(column_warp(col_base_ref[...], col_frac_ref[...]))
    warp_high[...] = high
    warp_low[...] = low
    factor = factor.astype(BF16)
    coverage = jnp.dot(factor, high, preferred_element_type=F32) + jnp.dot(factor, low, preferred_element_type=F32)
    for block in range(BLOCKS):
        cover[block] = coverage[:, block * LANES : (block + 1) * LANES]
    frac = column_of(frac_ref, (ROWS, LANES))
    spread = (1.0 - frac) + frac

    def one(s, carry):
        ry, rz = relative_patch(place, owner_ref[0, s])
        rows = pl.ds(offset_ref[0, s], ROWS)
        share = spread * weight_ref[0, s]
        for block in range(BLOCKS):
            sums[block, ry, rz, rows, :] += share * cover[block, pl.ds(s, 1), :]
        return carry

    lax.fori_loop(0, SEGS, one, 0, unroll=4)
    outputs = []
    for half in range(2):
        part = sums.at[2 * half : 2 * half + 2]
        outputs += write_out(place, part, keep.at[half], send.at[half], out_sems.at[half], U_ORDER[half])
    for copy in inputs[7:]:
        copy.wait()
    same = (
        lax.broadcasted_iota(jnp.int32, (BLOCK_ROWS, BLOCK_ROWS), 0) // ROWS
        == lax.broadcasted_iota(jnp.int32, (BLOCK_ROWS, BLOCK_ROWS), 1) // ROWS
    )
    for k in range(NBASIS):
        table = row_tables(bank_ref, index_ref, coeff_ref, base_ref, frac_ref, k)
        whole = jnp.where(same, jnp.concatenate([table] * BLOCK_SEGS, axis=0), 0.0)
        high, low = split(whole)
        rows = slice(k * BLOCK_ROWS, (k + 1) * BLOCK_ROWS)
        blockdiag[rows, 0:BLOCK_ROWS] = high
        blockdiag[rows, BLOCK_ROWS : 2 * BLOCK_ROWS] = high
        blockdiag[rows, 2 * BLOCK_ROWS :] = low
        profiles[k] = profile_row(bank_ref, index_ref, k)
    for copy in outputs:
        copy.wait()


def row_tables(bank_ref, index_ref, coeff_ref, base_ref, frac_ref, k):
    shape = (ROWS, BLOCK_ROWS)
    delta = lax.broadcasted_iota(jnp.int32, shape, 1) % ROWS - column_of(base_ref, shape) + REACH
    frac = column_of(frac_ref, shape)
    term = index_ref[0, k]
    lower = jnp.zeros(shape, F32)
    higher = jnp.zeros(shape, F32)
    for tap in range(TAPS):
        value = bank_ref[term, 0, tap]
        lower = jnp.where(delta == tap, value, lower)
        higher = jnp.where(delta == tap + 1, value, higher)
    return ((1.0 - frac) * lower + frac * higher) * coeff_ref[0, k]


def profile_row(bank_ref, index_ref, k):
    lane = lax.broadcasted_iota(jnp.int32, (8, WIDTH), 1)
    term = index_ref[0, k]
    row = jnp.zeros((8, WIDTH), F32)
    for tap in range(TAPS):
        row = jnp.where(lane == LANES + REACH - tap, bank_ref[term, 1, tap], row)
    return row


def band_tables(profile):
    return pltpu.roll(jnp.concatenate([profile] * (LANES // 8), axis=0), 0, 1, stride=1, stride_axis=0)[:, : 3 * LANES]


def rows_kernel(
    pixels_ref, factor_ref, blockdiag, profiles, u_high, u_low, near_high, near_low, cross_high, cross_low, done
):
    cross_high[...] = jnp.zeros(cross_high.shape, BF16)
    cross_low[...] = jnp.zeros(cross_low.shape, BF16)
    for k in range(NBASIS):
        for near, cross, band in zip(
            (near_high, near_low), (cross_high, cross_low), split(band_tables(profiles[k]))
        ):
            top = slice(k * HALF, k * HALF + LANES)
            bottom = slice(k * HALF + LANES, (k + 1) * HALF)
            left, middle, right = (band[:, i * LANES : (i + 1) * LANES] for i in range(3))
            near[top, :LANES] = middle
            near[top, LANES:] = right
            near[bottom, :LANES] = left
            near[bottom, LANES:] = middle
            cross[top, LANES:] = right
            cross[bottom, :LANES] = left
    def one(b, carry):
        segs = pl.ds(b * BLOCK_SEGS, BLOCK_SEGS)
        masked = (pixels_ref[0, segs] * factor_ref[segs, :][:, None, :]).reshape(BLOCK_ROWS, WIDTH)
        high, low = split(masked)
        product = jnp.dot(
            blockdiag[...], jnp.concatenate([high, low, high], axis=0), preferred_element_type=F32
        )
        rows = pl.ds(pl.multiple_of(b * BLOCK_ROWS, BLOCK_ROWS), BLOCK_ROWS)
        for k in range(NBASIS):
            part_high, part_low = split(product[k * BLOCK_ROWS : (k + 1) * BLOCK_ROWS])
            for half in range(2):
                of = slice(half * HALF, (half + 1) * HALF)
                u_high[half, rows, k * HALF : (k + 1) * HALF] = part_high[:, of]
                u_low[half, rows, k * HALF : (k + 1) * HALF] = part_low[:, of]
        return carry

    lax.fori_loop(0, SEGS // BLOCK_SEGS, one, 0, unroll=True)
    done[...] = jnp.zeros(done.shape, F32)


def put(place, owner_ref, offset_ref, weight_ref, lifted, first, sums):
    def one(s, carry):
        ry, rz = relative_patch(place, owner_ref[0, s])
        rows = pl.ds(offset_ref[0, s], ROWS)
        weight = weight_ref[0, s]
        of = pl.ds(pl.multiple_of(s * ROWS, ROWS), ROWS)
        for block in range(2):
            sums[block, ry, rz, rows, :] += weight * lifted[first + block, of, :]
        return carry

    lax.fori_loop(0, SEGS, one, 0, unroll=4)


def numer_kernel(
    owner_ref, offset_ref, weight_ref, warp_high, warp_low, u_high, u_low, near_high, near_low, cross_high, cross_low,
    after_0, after_1, keep, send, lifted, sums, y_high, y_low, sems,
):
    place = own_place()
    sums[...] = jnp.zeros(sums.shape, F32)
    dot = functools.partial(jnp.dot, preferred_element_type=F32)

    def one(b, carry):
        rows = pl.ds(pl.multiple_of(b * BLOCK_ROWS, BLOCK_ROWS), BLOCK_ROWS)
        part_high = u_high[:, rows, :].reshape(2 * BLOCK_ROWS, NBASIS * HALF)
        part_low = u_low[:, rows, :].reshape(2 * BLOCK_ROWS, NBASIS * HALF)
        near = dot(part_high, near_high[...]) + dot(part_high, near_low[...]) + dot(part_low, near_high[...])
        border_high, border_low = (
            jnp.concatenate(
                [
                    u[half, rows, k * HALF + (1 - half) * LANES : k * HALF + (2 - half) * LANES]
                    for k in range(NBASIS)
                    for half in range(2)
                ],
                axis=1,
            )
            for u in (u_high, u_low)
        )
        cross = (
            dot(border_high, cross_high[...]) + dot(border_high, cross_low[...]) + dot(border_low, cross_high[...])
        )
        left, right = near[:BLOCK_ROWS], near[BLOCK_ROWS:]
        wide = jnp.concatenate(
            [left[:, :LANES], left[:, LANES:] + cross[:, :LANES], right[:, :LANES] + cross[:, LANES:], right[:, LANES:]],
            axis=1,
        )
        high, low = split(wide)
        y_high[rows, :] = high
        y_low[rows, :] = low
        return carry

    lax.fori_loop(0, SEGS * ROWS // BLOCK_ROWS, one, 0, unroll=True)
    for half in range(2):
        cols = slice(half * HALF, (half + 1) * HALF)
        warped = (
            dot(y_high[...], warp_high[:, cols]) + dot(y_high[...], warp_low[:, cols])
            + dot(y_low[...], warp_high[:, cols])
        )
        lifted[2 * half] = warped[:, :LANES]
        lifted[2 * half + 1] = warped[:, LANES:]

    put(place, owner_ref, offset_ref, weight_ref, lifted, 0, sums)
    for copy in write_out(place, sums, keep, send, sems, U_ORDER[0]):
        copy.wait()


def second_kernel(owner_ref, offset_ref, weight_ref, lifted, keep, send, sums, sems):
    place = own_place()
    sums[...] = jnp.zeros(sums.shape, F32)
    put(place, owner_ref, offset_ref, weight_ref, lifted, 2, sums)
    for copy in write_out(place, sums, keep, send, sems, U_ORDER[1]):
        copy.wait()


SMEM = pl.BlockSpec(memory_space=pltpu.SMEM)
VMEM = pl.BlockSpec(memory_space=pltpu.VMEM)
ANY = pl.BlockSpec(memory_space=pl.ANY)
HBM = pl.BlockSpec(memory_space=pltpu.HBM)
TOKEN = jax.ShapeDtypeStruct((8, LANES), F32)
PARAMS = pltpu.CompilerParams(vmem_limit_bytes=40 * 1024 * 1024)


def pinned(*values):
    return [pltpu.with_memory_space_constraint(value, pltpu.HBM) for value in values]


def denom_sums(owner, offset, weight, bank, index, coeff, row_base, row_frac, bits, col_base, col_frac, pixels):
    parts = jax.ShapeDtypeStruct((2, 4, 4, 2, NZ, 8, LANES), F32)
    warp = jax.ShapeDtypeStruct((WIDTH, WIDTH), BF16)
    small = (owner, offset, weight, bank, index, coeff, row_base, row_frac)
    return pl.pallas_call(
        denom_kernel,
        out_shape=(
            parts, parts, jax.ShapeDtypeStruct(pixels.shape, F32), jax.ShapeDtypeStruct((SEGS, WIDTH), F32),
            jax.ShapeDtypeStruct((NBASIS * BLOCK_ROWS, 3 * BLOCK_ROWS), BF16),
            jax.ShapeDtypeStruct((NBASIS, 8, WIDTH), F32), warp, warp,
        ),
        in_specs=[HBM] * 12,
        out_specs=(ANY,) * 2 + (VMEM,) * 6,
        scratch_shapes=[pltpu.SMEM(value.shape, value.dtype) for value in small]
        + [pltpu.VMEM(value.shape, value.dtype) for value in (bits, col_base, col_frac)]
        + [
            pltpu.VMEM((BLOCKS, NY, NZ, 64, LANES), F32), pltpu.VMEM((BLOCKS, SEGS, LANES), F32),
            pltpu.SemaphoreType.DMA((12,)), pltpu.SemaphoreType.DMA((2, 32)),
        ],
        compiler_params=PARAMS,
        cost_estimate=pl.CostEstimate(flops=10**3, bytes_accessed=10**3, transcendentals=0),
        name="denom_sums",
    )(*(pltpu.with_memory_space_constraint(v, pltpu.HBM) for v in (*small, bits, col_base, col_frac, pixels)))


def row_pass(pixels, factor, blockdiag, profiles):
    band = jax.ShapeDtypeStruct((NBASIS * HALF, HALF), BF16)
    wide = jax.ShapeDtypeStruct((2, SEGS * ROWS, NBASIS * HALF), BF16)
    return pl.pallas_call(
        rows_kernel,
        out_shape=(wide, wide, band, band, band, band, TOKEN),
        in_specs=[VMEM] * 4,
        out_specs=(VMEM,) * 7,
        compiler_params=PARAMS,
        cost_estimate=pl.CostEstimate(flops=10**3, bytes_accessed=10**3, transcendentals=0),
        name="row_pass",
    )(pixels, factor, blockdiag, profiles)


PARTS = jax.ShapeDtypeStruct((4, 4, 2, NZ, 8, LANES), F32)
SUMS = pltpu.VMEM((2, NY, NZ, 64, LANES), F32)


def numer_sums(owner, offset, weight, warp, tables, after):
    wide = pltpu.VMEM((SEGS * ROWS, WIDTH), BF16)
    return pl.pallas_call(
        numer_kernel,
        out_shape=(PARTS, PARTS, jax.ShapeDtypeStruct((BLOCKS, SEGS * ROWS, LANES), F32)),
        in_specs=[SMEM] * 3 + [VMEM] * 10,
        out_specs=(ANY, ANY, VMEM),
        scratch_shapes=[SUMS, wide, wide, pltpu.SemaphoreType.DMA((32,))],
        compiler_params=PARAMS,
        cost_estimate=pl.CostEstimate(flops=10**3, bytes_accessed=10**3, transcendentals=0),
        name="numer_sums",
    )(owner, offset, weight, *warp, *tables, *after)


def second_sums(owner, offset, weight, lifted):
    return pl.pallas_call(
        second_kernel,
        out_shape=(PARTS, PARTS),
        in_specs=[SMEM] * 3 + [VMEM],
        out_specs=(ANY, ANY),
        scratch_shapes=[SUMS, pltpu.SemaphoreType.DMA((32,))],
        compiler_params=PARAMS,
        cost_estimate=pl.CostEstimate(flops=10**3, bytes_accessed=10**3, transcendentals=0),
        name="second_sums",
    )(owner, offset, weight, lifted)


def permute(value, partner):
    pairs = []
    for z in range(NZ):
        for y in range(NY):
            for x in range(NX):
                for core in range(2):
                    to_core, to_x, to_y, to_z = partner(core, x, y, z)
                    source = (z * NY + y) * 2 * NX + x * 2 + core
                    pairs.append((source, (to_z * NY + to_y) * 2 * NX + to_x * 2 + to_core))
    return lax.ppermute(value, ("sky", "grp"), pairs)


def swap_core(value):
    return permute(value, lambda core, x, y, z: (1 - core, x, y, z))


def swap_u(value, step):
    return permute(value, lambda core, x, y, z: (core, x, y ^ step, z) if core else (core, x ^ step, y, z))


def swap_v(value, step):
    return permute(value, lambda core, x, y, z: (core, x ^ step, y, z) if core else (core, x, y ^ step, z))


def swap_z(value, step):
    return permute(value, lambda core, x, y, z: (core, x, y, z ^ step))


def halve(keep, got):
    middle = keep.shape[0] // 2
    return keep[:middle] + got[:middle], keep[middle:] + got[middle:]


def hold(values, after):
    def kernel(*refs):
        pass

    return pl.pallas_call(
        kernel,
        out_shape=tuple(jax.ShapeDtypeStruct(value.shape, value.dtype) for value in values),
        in_specs=[VMEM] * (len(values) + len(after)),
        out_specs=(VMEM,) * len(values),
        input_output_aliases={i: i for i in range(len(values))},
        compiler_params=PARAMS,
        name="hold",
    )(*values, *after)


def per_device(
    pixels, mask_bits, owner, row_offset, seg_weight, psf_bank, basis_index, basis_coeff,
    row_base, row_frac, col_base, col_frac,
):
    d_keep, d_send, pixels, factor, blockdiag, profiles, *warp = denom_sums(
        owner, row_offset, seg_weight, psf_bank, basis_index, basis_coeff, row_base, row_frac,
        mask_bits, col_base, col_frac, pixels,
    )
    *tables, done = row_pass(pixels, factor, blockdiag, profiles)
    (d_got,) = hold((swap_core(d_send),), (done,))
    d_parts = [halve(d_keep[half], d_got[half]) for half in range(2)]
    keep_0, send_0, lifted = numer_sums(
        owner, row_offset, seg_weight, warp, tables, [send for _, send in d_parts]
    )
    keep_1, send_1 = second_sums(owner, row_offset, seg_weight, lifted)
    d_parts = [halve(keep, swap_u(send, step)) for (keep, send), step in zip(d_parts, (1, 3))]
    (send_1,) = hold((send_1,), [send for _, send in d_parts])
    n_parts = [halve(keep, swap_core(send)) for keep, send in ((keep_0, send_0), (keep_1, send_1))]
    d_parts = [keep[0] + swap_u(send, step)[0] for (keep, send), step in zip(d_parts, (3, 1))]
    n_parts = [halve(keep, swap_u(send, step)) for (keep, send), step in zip(n_parts, (1, 3))]
    n_parts = [keep[0] + swap_u(send, step)[0] for (keep, send), step in zip(n_parts, (3, 1))]
    both = jnp.concatenate(n_parts + d_parts, axis=1)
    both = both[0] + swap_v(both[1], 1) + swap_v(both[3], 3) + swap_v(both[2], 2)
    both = jnp.swapaxes(both, 0, 1)
    keep, send = halve(both[:4], swap_z(both[4:], 1))
    keep, send = halve(keep, swap_z(send, 2))
    both = (keep + swap_z(send, 4))[0]
    coadd = both[:BLOCKS] / jnp.maximum(both[BLOCKS:], 1.0)
    return jnp.swapaxes(coadd, 0, 1).reshape(8, WIDTH)


def solution(mesh):
    placed = (
        P("grp", "sky", None, None),
        P("grp", "sky", None),
        P("grp", "sky"),
        P("grp", "sky"),
        P("grp", "sky"),
        P(),
        P("grp", None),
        P("grp", None),
        P("grp", None),
        P("grp", None),
        P("grp", None),
        P("grp", None),
    )
    return jax.shard_map(
        per_device, mesh=mesh, in_specs=placed, out_specs=P(("sky", "grp"), None), check_vma=False
    )
```

```python
import functools

import jax
import jax.numpy as jnp
from jax import lax
from jax.experimental import pallas as pl
from jax.experimental.pallas import tpu as pltpu
from jax.sharding import PartitionSpec as P

F32 = jnp.float32
BF16 = jnp.bfloat16
NX, NY, NZ = 4, 4, 8
SEGS = 64
ROWS = 16
WIDTH = 512
TAPS = 21
REACH = 10
NBASIS = 3
LANES = 128
BLOCKS = WIDTH // LANES
HALF = WIDTH // 2
BLOCK_SEGS = 16
BLOCK_ROWS = BLOCK_SEGS * ROWS
EARLY = 1


def split(value):
    high = value.astype(BF16)
    return high, (value - high.astype(F32)).astype(BF16)


def column_factor(bits):
    bad = (bits & 1).astype(F32)
    full = ((bits >> 1) & 1).astype(F32)
    cosmic = ((bits >> 2) & 1).astype(F32)
    return (1.0 - bad) * (1.0 - 0.75 * full) * (1.0 - 0.5 * cosmic)


def column_warp(base, frac):
    source = lax.broadcasted_iota(jnp.int32, (WIDTH, base.shape[1]), 0)
    return jnp.where(source == base, 1.0 - frac, 0.0) + jnp.where(source == base + 1, frac, 0.0)


def column_of(ref, shape):
    row = lax.broadcasted_iota(jnp.int32, shape, 0)
    result = jnp.full(shape, ref[0, 0])
    for i in range(1, ROWS):
        result = jnp.where(row == i, ref[0, i], result)
    return result


A_FIRST = (0, 3, 1, 2)
B_FIRST = (0, 1, 3, 2)
U_ORDER = (A_FIRST, B_FIRST)
Z_ORDER = (0, 4, 2, 6, 1, 5, 3, 7)


def own_place():
    sky = lax.axis_index("sky")
    grp = lax.axis_index("grp")
    return grp % 2, grp // 2, sky % NY, sky // NY


def relative_patch(place, owner):
    ry = (owner % NY) ^ place[2]
    rz = (owner // NY) ^ place[3]
    return ry, (rz & 1) * 4 + ((rz >> 1) & 1) * 2 + (rz >> 2)


def write_out(place, sums, keep, send, sems, u_order):
    copies = []
    for to, core in ((keep, place[0]), (send, 1 - place[0])):
        for pu, ru in enumerate(u_order):
            for rv in range(4):
                rx = ru + core * (rv - ru)
                ry = rv + core * (ru - rv)
                rows = pl.ds(pl.multiple_of(((place[1] ^ rx) * 2 + core) * 8, 8), 8)
                copies.append(pltpu.make_async_copy(sums.at[:, ry, :, rows, :], to.at[pu, rv], sems.at[len(copies)]))
    for copy in copies:
        copy.start()
    return copies


def fetch(pairs, sems):
    copies = [pltpu.make_async_copy(src, dst, sems.at[i]) for i, (src, dst) in enumerate(pairs)]
    for copy in copies:
        copy.start()
    return copies


def denom_kernel(
    owner_hbm, offset_hbm, weight_hbm, bank_hbm, index_hbm, coeff_hbm, base_hbm, frac_hbm, bits_hbm,
    col_base_hbm, col_frac_hbm, pixels_hbm,
    keep, send, pixels_ref, factor_ref, blockdiag, profiles, warp_high, warp_low,
    owner_ref, offset_ref, weight_ref, bank_ref, index_ref, coeff_ref, base_ref, frac_ref, bits_ref,
    col_base_ref, col_frac_ref, sums, cover, sems, out_sems,
):
    place = own_place()
    inputs = fetch(
        (
            (owner_hbm, owner_ref), (offset_hbm, offset_ref), (weight_hbm, weight_ref),
            (frac_hbm, frac_ref), (bits_hbm, bits_ref), (col_base_hbm, col_base_ref), (col_frac_hbm, col_frac_ref),
            (bank_hbm, bank_ref), (index_hbm, index_ref), (coeff_hbm, coeff_ref), (base_hbm, base_ref),
            (pixels_hbm, pixels_ref),
        ),
        sems,
    )
    sums[...] = jnp.zeros(sums.shape, F32)
    for copy in inputs[:7]:
        copy.wait()
    factor = column_factor(bits_ref[0])
    factor_ref[...] = factor
    high, low = split(column_warp(col_base_ref[...], col_frac_ref[...]))
    warp_high[...] = high
    warp_low[...] = low
    factor = factor.astype(BF16)
    coverage = jnp.dot(factor, high, preferred_element_type=F32) + jnp.dot(factor, low, preferred_element_type=F32)
    for block in range(BLOCKS):
        cover[block] = coverage[:, block * LANES : (block + 1) * LANES]
    frac = column_of(frac_ref, (ROWS, LANES))
    spread = (1.0 - frac) + frac

    def one(s, carry):
        ry, rz = relative_patch(place, owner_ref[0, s])
        rows = pl.ds(offset_ref[0, s], ROWS)
        share = spread * weight_ref[0, s]
        for block in range(BLOCKS):
            sums[block, ry, rz, rows, :] += share * cover[block, pl.ds(s, 1), :]
        return carry

    lax.fori_loop(0, SEGS, one, 0, unroll=4)
    outputs = []
    for half in range(2):
        part = sums.at[2 * half : 2 * half + 2]
        outputs += write_out(place, part, keep.at[half], send.at[half], out_sems.at[half], U_ORDER[half])
    for copy in inputs[7:]:
        copy.wait()
    same = (
        lax.broadcasted_iota(jnp.int32, (BLOCK_ROWS, BLOCK_ROWS), 0) // ROWS
        == lax.broadcasted_iota(jnp.int32, (BLOCK_ROWS, BLOCK_ROWS), 1) // ROWS
    )
    for k in range(NBASIS):
        table = row_tables(bank_ref, index_ref, coeff_ref, base_ref, frac_ref, k)
        whole = jnp.where(same, jnp.concatenate([table] * BLOCK_SEGS, axis=0), 0.0)
        high, low = split(whole)
        rows = slice(k * BLOCK_ROWS, (k + 1) * BLOCK_ROWS)
        blockdiag[rows, 0:BLOCK_ROWS] = high
        blockdiag[rows, BLOCK_ROWS : 2 * BLOCK_ROWS] = high
        blockdiag[rows, 2 * BLOCK_ROWS :] = low
        profiles[k] = profile_row(bank_ref, index_ref, k)
    for copy in outputs:
        copy.wait()


def row_tables(bank_ref, index_ref, coeff_ref, base_ref, frac_ref, k):
    shape = (ROWS, BLOCK_ROWS)
    delta = lax.broadcasted_iota(jnp.int32, shape, 1) % ROWS - column_of(base_ref, shape) + REACH
    frac = column_of(frac_ref, shape)
    term = index_ref[0, k]
    lower = jnp.zeros(shape, F32)
    higher = jnp.zeros(shape, F32)
    for tap in range(TAPS):
        value = bank_ref[term, 0, tap]
        lower = jnp.where(delta == tap, value, lower)
        higher = jnp.where(delta == tap + 1, value, higher)
    return ((1.0 - frac) * lower + frac * higher) * coeff_ref[0, k]


def profile_row(bank_ref, index_ref, k):
    lane = lax.broadcasted_iota(jnp.int32, (8, WIDTH), 1)
    term = index_ref[0, k]
    row = jnp.zeros((8, WIDTH), F32)
    for tap in range(TAPS):
        row = jnp.where(lane == LANES + REACH - tap, bank_ref[term, 1, tap], row)
    return row


def band_tables(profile):
    return pltpu.roll(jnp.concatenate([profile] * (LANES // 8), axis=0), 0, 1, stride=1, stride_axis=0)[:, : 3 * LANES]


def column_pass(rows, u_high, u_low, bands, y_high, y_low):
    near_high, near_low, cross_high, cross_low = bands
    dot = functools.partial(jnp.dot, preferred_element_type=F32)
    part_high = u_high[:, rows, :].reshape(2 * BLOCK_ROWS, NBASIS * HALF)
    part_low = u_low[:, rows, :].reshape(2 * BLOCK_ROWS, NBASIS * HALF)
    near = dot(part_high, near_high[...]) + dot(part_high, near_low[...]) + dot(part_low, near_high[...])
    border_high, border_low = (
        jnp.concatenate(
            [
                u[half, rows, k * HALF + (1 - half) * LANES : k * HALF + (2 - half) * LANES]
                for k in range(NBASIS)
                for half in range(2)
            ],
            axis=1,
        )
        for u in (u_high, u_low)
    )
    cross = (
        dot(border_high, cross_high[...]) + dot(border_high, cross_low[...]) + dot(border_low, cross_high[...])
    )
    left, right = near[:BLOCK_ROWS], near[BLOCK_ROWS:]
    wide = jnp.concatenate(
        [left[:, :LANES], left[:, LANES:] + cross[:, :LANES], right[:, :LANES] + cross[:, LANES:], right[:, LANES:]],
        axis=1,
    )
    high, low = split(wide)
    y_high[rows, :] = high
    y_low[rows, :] = low


def rows_kernel(
    pixels_ref, factor_ref, blockdiag, profiles, y_high, y_low, u_high, u_low,
    near_high, near_low, cross_high, cross_low, done,
):
    cross_high[...] = jnp.zeros(cross_high.shape, BF16)
    cross_low[...] = jnp.zeros(cross_low.shape, BF16)
    for k in range(NBASIS):
        for near, cross, band in zip(
            (near_high, near_low), (cross_high, cross_low), split(band_tables(profiles[k]))
        ):
            top = slice(k * HALF, k * HALF + LANES)
            bottom = slice(k * HALF + LANES, (k + 1) * HALF)
            left, middle, right = (band[:, i * LANES : (i + 1) * LANES] for i in range(3))
            near[top, :LANES] = middle
            near[top, LANES:] = right
            near[bottom, :LANES] = left
            near[bottom, LANES:] = middle
            cross[top, LANES:] = right
            cross[bottom, :LANES] = left
    def one(b, carry):
        segs = pl.ds(b * BLOCK_SEGS, BLOCK_SEGS)
        masked = (pixels_ref[0, segs] * factor_ref[segs, :][:, None, :]).reshape(BLOCK_ROWS, WIDTH)
        high, low = split(masked)
        product = jnp.dot(
            blockdiag[...], jnp.concatenate([high, low, high], axis=0), preferred_element_type=F32
        )
        rows = pl.ds(pl.multiple_of(b * BLOCK_ROWS, BLOCK_ROWS), BLOCK_ROWS)
        for k in range(NBASIS):
            part_high, part_low = split(product[k * BLOCK_ROWS : (k + 1) * BLOCK_ROWS])
            for half in range(2):
                of = slice(half * HALF, (half + 1) * HALF)
                u_high[half, rows, k * HALF : (k + 1) * HALF] = part_high[:, of]
                u_low[half, rows, k * HALF : (k + 1) * HALF] = part_low[:, of]
        return carry

    lax.fori_loop(0, SEGS // BLOCK_SEGS, one, 0, unroll=True)
    for b in range(EARLY):
        rows = slice(b * BLOCK_ROWS, (b + 1) * BLOCK_ROWS)
        column_pass(rows, u_high, u_low, (near_high, near_low, cross_high, cross_low), y_high, y_low)
    done[...] = jnp.zeros(done.shape, F32)


def numer_kernel(
    owner_ref, offset_ref, weight_ref, warp_high, warp_low, early_high, early_low, u_high, u_low,
    near_high, near_low, cross_high, cross_low, after_0, after_1,
    keep_0, send_0, keep_1, send_1, sums, lifted, y_high, y_low, sems,
):
    place = own_place()
    sums[...] = jnp.zeros(sums.shape, F32)
    cut = EARLY * BLOCK_ROWS
    for b in range(EARLY, SEGS // BLOCK_SEGS):
        rows = slice(b * BLOCK_ROWS, (b + 1) * BLOCK_ROWS)
        column_pass(rows, u_high, u_low, (near_high, near_low, cross_high, cross_low), y_high, y_low)
    dot = functools.partial(jnp.dot, preferred_element_type=F32)
    for rows, high, low in ((slice(0, cut), early_high[...], early_low[...]), (slice(cut, None), y_high[cut:], y_low[cut:])):
        for half in range(2):
            cols = slice(half * HALF, (half + 1) * HALF)
            warped = dot(high, warp_high[:, cols]) + dot(high, warp_low[:, cols]) + dot(low, warp_high[:, cols])
            lifted[2 * half, rows] = warped[:, :LANES]
            lifted[2 * half + 1, rows] = warped[:, LANES:]

    def put(s, carry):
        ry, rz = relative_patch(place, owner_ref[0, s])
        rows = pl.ds(offset_ref[0, s], ROWS)
        weight = weight_ref[0, s]
        of = pl.ds(pl.multiple_of(s * ROWS, ROWS), ROWS)
        for block in range(BLOCKS):
            sums[block, ry, rz, rows, :] += weight * lifted[block, of, :]
        return carry

    lax.fori_loop(0, SEGS, put, 0, unroll=4)
    outputs = write_out(place, sums.at[0:2], keep_0, send_0, sems.at[0], U_ORDER[0])
    outputs += write_out(place, sums.at[2:4], keep_1, send_1, sems.at[1], U_ORDER[1])
    for copy in outputs:
        copy.wait()


SMEM = pl.BlockSpec(memory_space=pltpu.SMEM)
VMEM = pl.BlockSpec(memory_space=pltpu.VMEM)
ANY = pl.BlockSpec(memory_space=pl.ANY)
HBM = pl.BlockSpec(memory_space=pltpu.HBM)
TOKEN = jax.ShapeDtypeStruct((8, LANES), F32)
PARAMS = pltpu.CompilerParams(vmem_limit_bytes=24 * 1024 * 1024)


def pinned(*values):
    return [pltpu.with_memory_space_constraint(value, pltpu.HBM) for value in values]


def denom_sums(owner, offset, weight, bank, index, coeff, row_base, row_frac, bits, col_base, col_frac, pixels):
    parts = jax.ShapeDtypeStruct((2, 4, 4, 2, NZ, 8, LANES), F32)
    warp = jax.ShapeDtypeStruct((WIDTH, WIDTH), BF16)
    small = (owner, offset, weight, bank, index, coeff, row_base, row_frac)
    return pl.pallas_call(
        denom_kernel,
        out_shape=(
            parts, parts, jax.ShapeDtypeStruct(pixels.shape, F32), jax.ShapeDtypeStruct((SEGS, WIDTH), F32),
            jax.ShapeDtypeStruct((NBASIS * BLOCK_ROWS, 3 * BLOCK_ROWS), BF16),
            jax.ShapeDtypeStruct((NBASIS, 8, WIDTH), F32), warp, warp,
        ),
        in_specs=[HBM] * 12,
        out_specs=(ANY,) * 2 + (VMEM,) * 6,
        scratch_shapes=[pltpu.SMEM(value.shape, value.dtype) for value in small]
        + [pltpu.VMEM(value.shape, value.dtype) for value in (bits, col_base, col_frac)]
        + [
            pltpu.VMEM((BLOCKS, NY, NZ, 64, LANES), F32), pltpu.VMEM((BLOCKS, SEGS, LANES), F32),
            pltpu.SemaphoreType.DMA((12,)), pltpu.SemaphoreType.DMA((2, 32)),
        ],
        compiler_params=PARAMS,
        cost_estimate=pl.CostEstimate(flops=10**3, bytes_accessed=10**3, transcendentals=0),
        name="denom_sums",
    )(*(pltpu.with_memory_space_constraint(v, pltpu.HBM) for v in (*small, bits, col_base, col_frac, pixels)))


def row_pass(pixels, factor, blockdiag, profiles):
    early = jax.ShapeDtypeStruct((EARLY * BLOCK_ROWS, WIDTH), BF16)
    wide = jax.ShapeDtypeStruct((2, SEGS * ROWS, NBASIS * HALF), BF16)
    band = jax.ShapeDtypeStruct((NBASIS * HALF, HALF), BF16)
    return pl.pallas_call(
        rows_kernel,
        out_shape=(early, early, wide, wide, band, band, band, band, TOKEN),
        in_specs=[VMEM] * 4,
        out_specs=(VMEM,) * 9,
        compiler_params=PARAMS,
        cost_estimate=pl.CostEstimate(flops=10**3, bytes_accessed=10**3, transcendentals=0),
        name="row_pass",
    )(pixels, factor, blockdiag, profiles)


def numer_sums(owner, offset, weight, warp, tables, after):
    parts = jax.ShapeDtypeStruct((4, 4, 2, NZ, 8, LANES), F32)
    wide = pltpu.VMEM((SEGS * ROWS, WIDTH), BF16)
    return pl.pallas_call(
        numer_kernel,
        out_shape=(parts,) * 4,
        in_specs=[SMEM] * 3 + [VMEM] * 12,
        out_specs=(ANY,) * 4,
        scratch_shapes=[
            pltpu.VMEM((BLOCKS, NY, NZ, 64, LANES), F32), pltpu.VMEM((BLOCKS, SEGS * ROWS, LANES), F32),
            wide, wide, pltpu.SemaphoreType.DMA((2, 32)),
        ],
        compiler_params=PARAMS,
        cost_estimate=pl.CostEstimate(flops=10**3, bytes_accessed=10**3, transcendentals=0),
        name="numer_sums",
    )(owner, offset, weight, *warp, *tables, *after)


def permute(value, partner):
    pairs = []
    for z in range(NZ):
        for y in range(NY):
            for x in range(NX):
                for core in range(2):
                    to_core, to_x, to_y, to_z = partner(core, x, y, z)
                    source = (z * NY + y) * 2 * NX + x * 2 + core
                    pairs.append((source, (to_z * NY + to_y) * 2 * NX + to_x * 2 + to_core))
    return lax.ppermute(value, ("sky", "grp"), pairs)


def swap_core(value):
    return permute(value, lambda core, x, y, z: (1 - core, x, y, z))


def swap_u(value, step):
    return permute(value, lambda core, x, y, z: (core, x, y ^ step, z) if core else (core, x ^ step, y, z))


def swap_v(value, step):
    return permute(value, lambda core, x, y, z: (core, x ^ step, y, z) if core else (core, x, y ^ step, z))


def swap_z(value, step):
    return permute(value, lambda core, x, y, z: (core, x, y, z ^ step))


def halve(keep, got):
    middle = keep.shape[0] // 2
    return keep[:middle] + got[:middle], keep[middle:] + got[middle:]


def hold(values, after):
    def kernel(*refs):
        pass

    return pl.pallas_call(
        kernel,
        out_shape=tuple(jax.ShapeDtypeStruct(value.shape, value.dtype) for value in values),
        in_specs=[VMEM] * (len(values) + len(after)),
        out_specs=(VMEM,) * len(values),
        input_output_aliases={i: i for i in range(len(values))},
        compiler_params=PARAMS,
        name="hold",
    )(*values, *after)


def per_device(
    pixels, mask_bits, owner, row_offset, seg_weight, psf_bank, basis_index, basis_coeff,
    row_base, row_frac, col_base, col_frac,
):
    d_keep, d_send, pixels, factor, blockdiag, profiles, *warp = denom_sums(
        owner, row_offset, seg_weight, psf_bank, basis_index, basis_coeff, row_base, row_frac,
        mask_bits, col_base, col_frac, pixels,
    )
    *tables, done = row_pass(pixels, factor, blockdiag, profiles)
    (d_got,) = hold((swap_core(d_send),), (done,))
    d_parts = [halve(d_keep[half], d_got[half]) for half in range(2)]
    keep_0, send_0, keep_1, send_1 = numer_sums(
        owner, row_offset, seg_weight, warp, tables, [send for _, send in d_parts]
    )
    d_parts = [halve(keep, swap_u(send, step)) for (keep, send), step in zip(d_parts, (1, 3))]
    (send_1,) = hold((send_1,), [send for _, send in d_parts])
    n_parts = [halve(keep, swap_core(send)) for keep, send in ((keep_0, send_0), (keep_1, send_1))]
    d_parts = [keep[0] + swap_u(send, step)[0] for (keep, send), step in zip(d_parts, (3, 1))]
    n_parts = [halve(keep, swap_u(send, step)) for (keep, send), step in zip(n_parts, (1, 3))]
    n_parts = [keep[0] + swap_u(send, step)[0] for (keep, send), step in zip(n_parts, (3, 1))]
    both = jnp.concatenate(n_parts + d_parts, axis=1)
    both = both[0] + swap_v(both[1], 1) + swap_v(both[3], 3) + swap_v(both[2], 2)
    both = jnp.swapaxes(both, 0, 1)
    keep, send = halve(both[:4], swap_z(both[4:], 1))
    keep, send = halve(keep, swap_z(send, 2))
    both = (keep + swap_z(send, 4))[0]
    coadd = both[:BLOCKS] / jnp.maximum(both[BLOCKS:], 1.0)
    return jnp.swapaxes(coadd, 0, 1).reshape(8, WIDTH)


def solution(mesh):
    placed = (
        P("grp", "sky", None, None),
        P("grp", "sky", None),
        P("grp", "sky"),
        P("grp", "sky"),
        P("grp", "sky"),
        P(),
        P("grp", None),
        P("grp", None),
        P("grp", None),
        P("grp", None),
        P("grp", None),
        P("grp", None),
    )
    return jax.shard_map(
        per_device, mesh=mesh, in_specs=placed, out_specs=P(("sky", "grp"), None), check_vma=False
    )
```

```python
import functools

import jax
import jax.numpy as jnp
from jax import lax
from jax.experimental import pallas as pl
from jax.experimental.pallas import tpu as pltpu
from jax.sharding import PartitionSpec as P

F32 = jnp.float32
BF16 = jnp.bfloat16
NX, NY, NZ = 4, 4, 8
SEGS = 64
ROWS = 16
WIDTH = 512
TAPS = 21
REACH = 10
NBASIS = 3
LANES = 128
BLOCKS = WIDTH // LANES
HALF = WIDTH // 2
BLOCK_SEGS = 16
BLOCK_ROWS = BLOCK_SEGS * ROWS
EARLY = 1


def split(value):
    high = value.astype(BF16)
    return high, (value - high.astype(F32)).astype(BF16)


def column_factor(bits):
    bad = (bits & 1).astype(F32)
    full = ((bits >> 1) & 1).astype(F32)
    cosmic = ((bits >> 2) & 1).astype(F32)
    return (1.0 - bad) * (1.0 - 0.75 * full) * (1.0 - 0.5 * cosmic)


def column_warp(base, frac):
    source = lax.broadcasted_iota(jnp.int32, (WIDTH, base.shape[1]), 0)
    return jnp.where(source == base, 1.0 - frac, 0.0) + jnp.where(source == base + 1, frac, 0.0)


def column_of(ref, shape):
    row = lax.broadcasted_iota(jnp.int32, shape, 0)
    result = jnp.full(shape, ref[0, 0])
    for i in range(1, ROWS):
        result = jnp.where(row == i, ref[0, i], result)
    return result


A_FIRST = (0, 3, 1, 2)
B_FIRST = (0, 1, 3, 2)
U_ORDER = (A_FIRST, B_FIRST)
Z_ORDER = (0, 4, 2, 6, 1, 5, 3, 7)


def own_place():
    sky = lax.axis_index("sky")
    grp = lax.axis_index("grp")
    return grp % 2, grp // 2, sky % NY, sky // NY


def relative_patch(place, owner):
    ry = (owner % NY) ^ place[2]
    rz = (owner // NY) ^ place[3]
    return ry, (rz & 1) * 4 + ((rz >> 1) & 1) * 2 + (rz >> 2)


def write_out(place, sums, keep, send, sems, u_order):
    copies = []
    for to, core in ((keep, place[0]), (send, 1 - place[0])):
        for pu, ru in enumerate(u_order):
            for rv in range(4):
                rx = ru + core * (rv - ru)
                ry = rv + core * (ru - rv)
                rows = pl.ds(pl.multiple_of(((place[1] ^ rx) * 2 + core) * 8, 8), 8)
                copies.append(pltpu.make_async_copy(sums.at[:, ry, :, rows, :], to.at[pu, rv], sems.at[len(copies)]))
    for copy in copies:
        copy.start()
    return copies


def fetch(pairs, sems):
    copies = [pltpu.make_async_copy(src, dst, sems.at[i]) for i, (src, dst) in enumerate(pairs)]
    for copy in copies:
        copy.start()
    return copies


def denom_kernel(
    owner_hbm, offset_hbm, weight_hbm, bank_hbm, index_hbm, coeff_hbm, base_hbm, frac_hbm, bits_hbm,
    col_base_hbm, col_frac_hbm, pixels_hbm,
    keep, send, pixels_ref, factor_ref, blockdiag, profiles, warp_high, warp_low,
    owner_ref, offset_ref, weight_ref, bank_ref, index_ref, coeff_ref, base_ref, frac_ref, bits_ref,
    col_base_ref, col_frac_ref, sums, cover, sems, out_sems,
):
    place = own_place()
    inputs = fetch(
        (
            (owner_hbm, owner_ref), (offset_hbm, offset_ref), (weight_hbm, weight_ref),
            (frac_hbm, frac_ref), (bits_hbm, bits_ref), (col_base_hbm, col_base_ref), (col_frac_hbm, col_frac_ref),
            (bank_hbm, bank_ref), (index_hbm, index_ref), (coeff_hbm, coeff_ref), (base_hbm, base_ref),
            (pixels_hbm, pixels_ref),
        ),
        sems,
    )
    sums[...] = jnp.zeros(sums.shape, F32)
    for copy in inputs[:7]:
        copy.wait()
    factor = column_factor(bits_ref[0])
    factor_ref[...] = factor
    high, low = split(column_warp(col_base_ref[...], col_frac_ref[...]))
    warp_high[...] = high
    warp_low[...] = low
    factor = factor.astype(BF16)
    coverage = jnp.dot(factor, high, preferred_element_type=F32) + jnp.dot(factor, low, preferred_element_type=F32)
    for block in range(BLOCKS):
        cover[block] = coverage[:, block * LANES : (block + 1) * LANES]
    frac = column_of(frac_ref, (ROWS, LANES))
    spread = (1.0 - frac) + frac

    def one(s, carry):
        ry, rz = relative_patch(place, owner_ref[0, s])
        rows = pl.ds(offset_ref[0, s], ROWS)
        share = spread * weight_ref[0, s]
        for block in range(BLOCKS):
            sums[block, ry, rz, rows, :] += share * cover[block, pl.ds(s, 1), :]
        return carry

    lax.fori_loop(0, SEGS, one, 0, unroll=4)
    outputs = []
    for half in range(2):
        part = sums.at[2 * half : 2 * half + 2]
        outputs += write_out(place, part, keep.at[half], send.at[half], out_sems.at[half], U_ORDER[half])
    for copy in inputs[7:]:
        copy.wait()
    same = (
        lax.broadcasted_iota(jnp.int32, (BLOCK_ROWS, BLOCK_ROWS), 0) // ROWS
        == lax.broadcasted_iota(jnp.int32, (BLOCK_ROWS, BLOCK_ROWS), 1) // ROWS
    )
    for k in range(NBASIS):
        table = row_tables(bank_ref, index_ref, coeff_ref, base_ref, frac_ref, k)
        whole = jnp.where(same, jnp.concatenate([table] * BLOCK_SEGS, axis=0), 0.0)
        high, low = split(whole)
        rows = slice(k * BLOCK_ROWS, (k + 1) * BLOCK_ROWS)
        blockdiag[rows, 0:BLOCK_ROWS] = high
        blockdiag[rows, BLOCK_ROWS : 2 * BLOCK_ROWS] = high
        blockdiag[rows, 2 * BLOCK_ROWS :] = low
        profiles[k] = profile_row(bank_ref, index_ref, k)
    for copy in outputs:
        copy.wait()


def row_tables(bank_ref, index_ref, coeff_ref, base_ref, frac_ref, k):
    shape = (ROWS, BLOCK_ROWS)
    delta = lax.broadcasted_iota(jnp.int32, shape, 1) % ROWS - column_of(base_ref, shape) + REACH
    frac = column_of(frac_ref, shape)
    term = index_ref[0, k]
    lower = jnp.zeros(shape, F32)
    higher = jnp.zeros(shape, F32)
    for tap in range(TAPS):
        value = bank_ref[term, 0, tap]
        lower = jnp.where(delta == tap, value, lower)
        higher = jnp.where(delta == tap + 1, value, higher)
    return ((1.0 - frac) * lower + frac * higher) * coeff_ref[0, k]


def profile_row(bank_ref, index_ref, k):
    lane = lax.broadcasted_iota(jnp.int32, (8, WIDTH), 1)
    term = index_ref[0, k]
    row = jnp.zeros((8, WIDTH), F32)
    for tap in range(TAPS):
        row = jnp.where(lane == LANES + REACH - tap, bank_ref[term, 1, tap], row)
    return row


def band_tables(profile):
    return pltpu.roll(jnp.concatenate([profile] * (LANES // 8), axis=0), 0, 1, stride=1, stride_axis=0)[:, : 3 * LANES]


def column_pass(rows, u_high, u_low, bands, y_high, y_low):
    near_high, near_low, cross_high, cross_low = bands
    dot = functools.partial(jnp.dot, preferred_element_type=F32)
    part_high = u_high[:, rows, :].reshape(2 * BLOCK_ROWS, NBASIS * HALF)
    part_low = u_low[:, rows, :].reshape(2 * BLOCK_ROWS, NBASIS * HALF)
    near = dot(part_high, near_high[...]) + dot(part_high, near_low[...]) + dot(part_low, near_high[...])
    upper = lax.broadcasted_iota(jnp.int32, (BLOCK_ROWS, LANES), 1) < LANES // 2
    border_high, border_low = (
        jnp.concatenate(
            [
                jnp.where(upper, u[1, rows, k * HALF : k * HALF + LANES], u[0, rows, k * HALF + LANES : (k + 1) * HALF])
                for k in range(NBASIS)
            ],
            axis=1,
        )
        for u in (u_high, u_low)
    )
    cross = (
        dot(border_high, cross_high[...]) + dot(border_high, cross_low[...]) + dot(border_low, cross_high[...])
    )
    left, right = near[:BLOCK_ROWS], near[BLOCK_ROWS:]
    wide = jnp.concatenate(
        [left[:, :LANES], left[:, LANES:] + cross[:, :LANES], right[:, :LANES] + cross[:, LANES:], right[:, LANES:]],
        axis=1,
    )
    high, low = split(wide)
    y_high[rows, :] = high
    y_low[rows, :] = low


def rows_kernel(
    pixels_ref, factor_ref, blockdiag, profiles, y_high, y_low, u_high, u_low,
    near_high, near_low, cross_high, cross_low, done,
):
    upper = lax.broadcasted_iota(jnp.int32, (LANES, LANES), 0) < LANES // 2
    for k in range(NBASIS):
        band = band_tables(profiles[k])
        left, middle, right = (band[:, i * LANES : (i + 1) * LANES] for i in range(3))
        rows = slice(k * HALF, (k + 1) * HALF)
        whole = jnp.concatenate([jnp.concatenate([middle, right], axis=1), jnp.concatenate([left, middle], axis=1)])
        near_high[rows, :], near_low[rows, :] = split(whole)
        rows = slice(k * LANES, (k + 1) * LANES)
        border = jnp.concatenate([jnp.where(upper, left, 0.0), jnp.where(upper, 0.0, right)], axis=1)
        cross_high[rows, :], cross_low[rows, :] = split(border)

    def one(b, carry):
        segs = pl.ds(b * BLOCK_SEGS, BLOCK_SEGS)
        masked = (pixels_ref[0, segs] * factor_ref[segs, :][:, None, :]).reshape(BLOCK_ROWS, WIDTH)
        high, low = split(masked)
        product = jnp.dot(
            blockdiag[...], jnp.concatenate([high, low, high], axis=0), preferred_element_type=F32
        )
        rows = pl.ds(pl.multiple_of(b * BLOCK_ROWS, BLOCK_ROWS), BLOCK_ROWS)
        for k in range(NBASIS):
            part_high, part_low = split(product[k * BLOCK_ROWS : (k + 1) * BLOCK_ROWS])
            for half in range(2):
                of = slice(half * HALF, (half + 1) * HALF)
                u_high[half, rows, k * HALF : (k + 1) * HALF] = part_high[:, of]
                u_low[half, rows, k * HALF : (k + 1) * HALF] = part_low[:, of]
        return carry

    lax.fori_loop(0, SEGS // BLOCK_SEGS, one, 0, unroll=True)
    for b in range(EARLY):
        rows = slice(b * BLOCK_ROWS, (b + 1) * BLOCK_ROWS)
        column_pass(rows, u_high, u_low, (near_high, near_low, cross_high, cross_low), y_high, y_low)
    done[...] = jnp.zeros(done.shape, F32)


def numer_kernel(
    owner_ref, offset_ref, weight_ref, warp_high, warp_low, early_high, early_low, u_high, u_low,
    near_high, near_low, cross_high, cross_low, after_0, after_1,
    keep_0, send_0, keep_1, send_1, sums, lifted, y_high, y_low, sems,
):
    place = own_place()
    sums[...] = jnp.zeros(sums.shape, F32)
    cut = EARLY * BLOCK_ROWS
    for b in range(EARLY, SEGS // BLOCK_SEGS):
        rows = slice(b * BLOCK_ROWS, (b + 1) * BLOCK_ROWS)
        column_pass(rows, u_high, u_low, (near_high, near_low, cross_high, cross_low), y_high, y_low)
    dot = functools.partial(jnp.dot, preferred_element_type=F32)
    for rows, high, low in ((slice(0, cut), early_high[...], early_low[...]), (slice(cut, None), y_high[cut:], y_low[cut:])):
        for half in range(2):
            cols = slice(half * HALF, (half + 1) * HALF)
            warped = dot(high, warp_high[:, cols]) + dot(high, warp_low[:, cols]) + dot(low, warp_high[:, cols])
            lifted[2 * half, rows] = warped[:, :LANES]
            lifted[2 * half + 1, rows] = warped[:, LANES:]

    def put(s, carry):
        ry, rz = relative_patch(place, owner_ref[0, s])
        rows = pl.ds(offset_ref[0, s], ROWS)
        weight = weight_ref[0, s]
        of = pl.ds(pl.multiple_of(s * ROWS, ROWS), ROWS)
        for block in range(BLOCKS):
            sums[block, ry, rz, rows, :] += weight * lifted[block, of, :]
        return carry

    lax.fori_loop(0, SEGS, put, 0, unroll=4)
    outputs = write_out(place, sums.at[0:2], keep_0, send_0, sems.at[0], U_ORDER[0])
    outputs += write_out(place, sums.at[2:4], keep_1, send_1, sems.at[1], U_ORDER[1])
    for copy in outputs:
        copy.wait()


SMEM = pl.BlockSpec(memory_space=pltpu.SMEM)
VMEM = pl.BlockSpec(memory_space=pltpu.VMEM)
ANY = pl.BlockSpec(memory_space=pl.ANY)
HBM = pl.BlockSpec(memory_space=pltpu.HBM)
TOKEN = jax.ShapeDtypeStruct((8, LANES), F32)
PARAMS = pltpu.CompilerParams(vmem_limit_bytes=24 * 1024 * 1024)


def pinned(*values):
    return [pltpu.with_memory_space_constraint(value, pltpu.HBM) for value in values]


def denom_sums(owner, offset, weight, bank, index, coeff, row_base, row_frac, bits, col_base, col_frac, pixels):
    parts = jax.ShapeDtypeStruct((2, 4, 4, 2, NZ, 8, LANES), F32)
    warp = jax.ShapeDtypeStruct((WIDTH, WIDTH), BF16)
    small = (owner, offset, weight, bank, index, coeff, row_base, row_frac)
    return pl.pallas_call(
        denom_kernel,
        out_shape=(
            parts, parts, jax.ShapeDtypeStruct(pixels.shape, F32), jax.ShapeDtypeStruct((SEGS, WIDTH), F32),
            jax.ShapeDtypeStruct((NBASIS * BLOCK_ROWS, 3 * BLOCK_ROWS), BF16),
            jax.ShapeDtypeStruct((NBASIS, 8, WIDTH), F32), warp, warp,
        ),
        in_specs=[HBM] * 12,
        out_specs=(ANY,) * 2 + (VMEM,) * 6,
        scratch_shapes=[pltpu.SMEM(value.shape, value.dtype) for value in small]
        + [pltpu.VMEM(value.shape, value.dtype) for value in (bits, col_base, col_frac)]
        + [
            pltpu.VMEM((BLOCKS, NY, NZ, 64, LANES), F32), pltpu.VMEM((BLOCKS, SEGS, LANES), F32),
            pltpu.SemaphoreType.DMA((12,)), pltpu.SemaphoreType.DMA((2, 32)),
        ],
        compiler_params=PARAMS,
        cost_estimate=pl.CostEstimate(flops=10**3, bytes_accessed=10**3, transcendentals=0),
        name="denom_sums",
    )(*(pltpu.with_memory_space_constraint(v, pltpu.HBM) for v in (*small, bits, col_base, col_frac, pixels)))


def row_pass(pixels, factor, blockdiag, profiles):
    early = jax.ShapeDtypeStruct((EARLY * BLOCK_ROWS, WIDTH), BF16)
    wide = jax.ShapeDtypeStruct((2, SEGS * ROWS, NBASIS * HALF), BF16)
    band = jax.ShapeDtypeStruct((NBASIS * HALF, HALF), BF16)
    cross = jax.ShapeDtypeStruct((NBASIS * LANES, HALF), BF16)
    return pl.pallas_call(
        rows_kernel,
        out_shape=(early, early, wide, wide, band, band, cross, cross, TOKEN),
        in_specs=[VMEM] * 4,
        out_specs=(VMEM,) * 9,
        compiler_params=PARAMS,
        cost_estimate=pl.CostEstimate(flops=10**3, bytes_accessed=10**3, transcendentals=0),
        name="row_pass",
    )(pixels, factor, blockdiag, profiles)


def numer_sums(owner, offset, weight, warp, tables, after):
    parts = jax.ShapeDtypeStruct((4, 4, 2, NZ, 8, LANES), F32)
    wide = pltpu.VMEM((SEGS * ROWS, WIDTH), BF16)
    return pl.pallas_call(
        numer_kernel,
        out_shape=(parts,) * 4,
        in_specs=[SMEM] * 3 + [VMEM] * 12,
        out_specs=(ANY,) * 4,
        scratch_shapes=[
            pltpu.VMEM((BLOCKS, NY, NZ, 64, LANES), F32), pltpu.VMEM((BLOCKS, SEGS * ROWS, LANES), F32),
            wide, wide, pltpu.SemaphoreType.DMA((2, 32)),
        ],
        compiler_params=PARAMS,
        cost_estimate=pl.CostEstimate(flops=10**3, bytes_accessed=10**3, transcendentals=0),
        name="numer_sums",
    )(owner, offset, weight, *warp, *tables, *after)


def permute(value, partner):
    pairs = []
    for z in range(NZ):
        for y in range(NY):
            for x in range(NX):
                for core in range(2):
                    to_core, to_x, to_y, to_z = partner(core, x, y, z)
                    source = (z * NY + y) * 2 * NX + x * 2 + core
                    pairs.append((source, (to_z * NY + to_y) * 2 * NX + to_x * 2 + to_core))
    return lax.ppermute(value, ("sky", "grp"), pairs)


def swap_core(value):
    return permute(value, lambda core, x, y, z: (1 - core, x, y, z))


def swap_u(value, step):
    return permute(value, lambda core, x, y, z: (core, x, y ^ step, z) if core else (core, x ^ step, y, z))


def swap_v(value, step):
    return permute(value, lambda core, x, y, z: (core, x ^ step, y, z) if core else (core, x, y ^ step, z))


def swap_z(value, step):
    return permute(value, lambda core, x, y, z: (core, x, y, z ^ step))


def halve(keep, got):
    middle = keep.shape[0] // 2
    return keep[:middle] + got[:middle], keep[middle:] + got[middle:]


def hold(values, after):
    def kernel(*refs):
        pass

    return pl.pallas_call(
        kernel,
        out_shape=tuple(jax.ShapeDtypeStruct(value.shape, value.dtype) for value in values),
        in_specs=[VMEM] * (len(values) + len(after)),
        out_specs=(VMEM,) * len(values),
        input_output_aliases={i: i for i in range(len(values))},
        compiler_params=PARAMS,
        name="hold",
    )(*values, *after)


def per_device(
    pixels, mask_bits, owner, row_offset, seg_weight, psf_bank, basis_index, basis_coeff,
    row_base, row_frac, col_base, col_frac,
):
    d_keep, d_send, pixels, factor, blockdiag, profiles, *warp = denom_sums(
        owner, row_offset, seg_weight, psf_bank, basis_index, basis_coeff, row_base, row_frac,
        mask_bits, col_base, col_frac, pixels,
    )
    *tables, done = row_pass(pixels, factor, blockdiag, profiles)
    (d_got,) = hold((swap_core(d_send),), (done,))
    d_parts = [halve(d_keep[half], d_got[half]) for half in range(2)]
    keep_0, send_0, keep_1, send_1 = numer_sums(
        owner, row_offset, seg_weight, warp, tables, [send for _, send in d_parts]
    )
    d_parts = [halve(keep, swap_u(send, step)) for (keep, send), step in zip(d_parts, (1, 3))]
    (send_1,) = hold((send_1,), [send for _, send in d_parts])
    n_parts = [halve(keep, swap_core(send)) for keep, send in ((keep_0, send_0), (keep_1, send_1))]
    d_parts = [keep[0] + swap_u(send, step)[0] for (keep, send), step in zip(d_parts, (3, 1))]
    n_parts = [halve(keep, swap_u(send, step)) for (keep, send), step in zip(n_parts, (1, 3))]
    n_parts = [keep[0] + swap_u(send, step)[0] for (keep, send), step in zip(n_parts, (3, 1))]
    both = jnp.concatenate(n_parts + d_parts, axis=1)
    both = both[0] + swap_v(both[1], 1) + swap_v(both[3], 3) + swap_v(both[2], 2)
    both = jnp.swapaxes(both, 0, 1)
    keep, send = halve(both[:4], swap_z(both[4:], 1))
    keep, send = halve(keep, swap_z(send, 2))
    both = (keep + swap_z(send, 4))[0]
    coadd = both[:BLOCKS] / jnp.maximum(both[BLOCKS:], 1.0)
    return jnp.swapaxes(coadd, 0, 1).reshape(8, WIDTH)


def solution(mesh):
    placed = (
        P("grp", "sky", None, None),
        P("grp", "sky", None),
        P("grp", "sky"),
        P("grp", "sky"),
        P("grp", "sky"),
        P(),
        P("grp", None),
        P("grp", None),
        P("grp", None),
        P("grp", None),
        P("grp", None),
        P("grp", None),
    )
    return jax.shard_map(
        per_device, mesh=mesh, in_specs=placed, out_specs=P(("sky", "grp"), None), check_vma=False
    )
```
